256 devices in a mesh: dp: 2 (over core), fsdp: 8 (over z_lo, y), tensor: 16 (over z_hi, x).
Axes of the slice: x: 4, y: 4, z: 8 (z_hi: 4, z_lo: 2; z = z_hi * 2 + z_lo), core: 2. Of those that a mesh axis runs over, the one named last changes fastest.
Arguments:
- replica_grads: bfloat16 [2, 3584, 10240], P('dp', 'fsdp', 'tensor'), may hold values from -6 to 6
- basis_left: bfloat16 [3584, 3584], P('fsdp'), may hold values from -0.09375 to 0.09375
- basis_right: bfloat16 [10240, 10240], P('fsdp', 'tensor'), may hold values from -0.0625 to 0.0625
- first_moment: float32 [3584, 10240], P(('dp', 'fsdp'), 'tensor'), may hold values from -6 to 6
- second_moment: float32 [3584, 10240], P(('dp', 'fsdp'), 'tensor'), may hold values from 0.5 to 4
Outputs:
- first_next: float32 [3584, 10240], P(('dp', 'fsdp'), 'tensor')
- second_next: float32 [3584, 10240], P(('dp', 'fsdp'), 'tensor')
- update: float32 [3584, 10240], P('fsdp', 'tensor')
The draws below stay inside these ranges and needn't reach their ends.
All inputs are finite; a program needn't handle non-finite values.
Results may differ from the reference program's by a relative error of at most 0.02.
Values may be sent and summed in bfloat16 or wider, within the bound.
A program may use at most 128 MiB of HBM per device.

```python
import math
import jax
import jax.numpy as jnp
from jax import lax

D = 3584
F = 10240
ADAM_STEP = 10
N_DP = 2
N_FSDP = 8
N_TENSOR = 16


def levels(rng, shape, split, low, high):
    def one(position, blocks):
        heights = jax.random.uniform(jax.random.fold_in(jax.random.fold_in(rng, 6), position), (blocks,), jnp.float32, low / len(split), high / len(split))
        return jnp.repeat(jnp.exp(heights), shape[position] // blocks).reshape((-1,) + (1,) * (len(shape) - position - 1))

    loudness = one(*split[0])
    for cut in split[1:]:
        loudness = loudness * one(*cut)
    return loudness


def noise(stream_key, extent, scale, reach, pieces=(), held_as=jnp.bfloat16):
    array = jax.random.normal(stream_key, extent, jnp.float32) * scale
    if len(pieces) > 0:
        array = levels(stream_key, extent, pieces, -0.22, 0.18) * array
    return jnp.clip(array, min=-reach, max=reach).astype(held_as)


def setup_inputs(seed: int = 0) -> dict:
    streams_of = jax.random.split(jax.random.key(seed), 6)
    replica_grads = noise(streams_of[0], (N_DP, D, F), 1.0, 6.0, ((0, 2), (1, 8), (2, 16)))
    basis_left = noise(streams_of[1], (D, D), D ** -0.5, 0.09375, ((0, 8),))
    basis_right = noise(streams_of[2], (F, F), F ** -0.5, 0.0625, ((0, 8), (1, 16)))
    first_moment = noise(streams_of[3], (D, F), 1.0, 6.0, ((0, 16), (1, 16)), jnp.float32)
    second_moment = jnp.clip(jnp.exp(math.log(4.0) - 2.0794415 * jax.random.uniform(streams_of[4], (D, F), jnp.float32) ** levels(streams_of[4], (D, F), ((0, 16), (1, 16)), -0.2, 0.2)), 0.5, 4.0)
    return {"replica_grads": replica_grads, "basis_left": basis_left, "basis_right": basis_right, "first_moment": first_moment, "second_moment": second_moment}


beta_first = 0.9
beta_second = 0.95
epsilon = 1e-08

def rotate_left_side(basis_left, gradient):
    block_rows = D // (N_DP * N_FSDP)

    def add_block(running, block_index):
        offset = (block_index * block_rows).astype(jnp.int32)
        basis_part = lax.dynamic_slice_in_dim(basis_left, offset, block_rows, 0)
        grad_part = lax.dynamic_slice_in_dim(gradient, offset, block_rows, 0)
        partial_sum = lax.dot_general(basis_part, grad_part, (((0,), (0,)), ((), ())), preferred_element_type=jnp.float32)
        rounded = lax.optimization_barrier(partial_sum.astype(jnp.bfloat16))
        return (running + rounded.astype(jnp.float32), None)
    summed_up, unused = lax.scan(add_block, jnp.zeros((D, F), jnp.float32), jnp.arange(N_DP * N_FSDP, dtype=jnp.int32))
    return summed_up.astype(jnp.bfloat16)

def rotate_back_right(direction, basis_right):
    block_cols = F // N_TENSOR

    def add_block(running, block_index):
        offset = (block_index * block_cols).astype(jnp.int32)
        dir_part = lax.dynamic_slice_in_dim(direction, offset, block_cols, 1)
        basis_part = lax.dynamic_slice_in_dim(basis_right, offset, block_cols, 1)
        partial_sum = lax.dot_general(dir_part, basis_part, (((1,), (1,)), ((), ())), preferred_element_type=jnp.float32)
        rounded = lax.optimization_barrier(partial_sum.astype(jnp.bfloat16))
        return (running + rounded.astype(jnp.float32), None)
    summed_up, unused = lax.scan(add_block, jnp.zeros((D, F), jnp.float32), jnp.arange(N_TENSOR, dtype=jnp.int32))
    return summed_up.astype(jnp.bfloat16)

def reference(replica_grads, basis_left, basis_right, first_moment, second_moment):
    summed = lax.optimization_barrier(jnp.sum(replica_grads.astype(jnp.float32), axis=0))
    gradient = summed.astype(jnp.bfloat16)
    rot_left = rotate_left_side(basis_left, gradient)
    rotated = jnp.dot(rot_left, basis_right, preferred_element_type=jnp.float32)
    first_next = beta_first * first_moment + (1.0 - beta_first) * rotated
    second_next = beta_second * second_moment + (1.0 - beta_second) * rotated * rotated
    first_hat = first_next / (1.0 - beta_first ** ADAM_STEP)
    second_hat = second_next / (1.0 - beta_second ** ADAM_STEP)
    direction = (first_hat / (jnp.sqrt(second_hat) + epsilon)).astype(jnp.bfloat16)
    back_right = rotate_back_right(direction, basis_right)
    update = jnp.dot(basis_left, back_right, preferred_element_type=jnp.float32)
    return (first_next, second_next, update)
```

```python
import functools

import jax
import jax.numpy as jnp
from jax import lax
from jax.experimental import pallas as pl
from jax.experimental.pallas import tpu as pltpu
from jax.sharding import PartitionSpec as P

MESH = pl.DeviceIdType.MESH
F32 = jnp.float32
BF16 = jnp.bfloat16

ADAM_STEP = 10
beta_first = 0.9
beta_second = 0.95
epsilon = 1e-08

ROWS = 448
HALF = 224
COLS = 640
SUB = 112


class Ids:
    def __init__(self):
        self.table = {}
        self.count = 0

    def get(self, name, width=1):
        if name not in self.table:
            self.table[name] = self.count
            self.count += width
        return self.table[name]


def kernel(
    g_hbm, ql_hbm, qr_hbm, m1_hbm, m2_hbm,
    o1_hbm, o2_hbm, up_hbm,
    gv, gx, gs, G, Q, QL, T, Ts, Tr, Tb, Pb, Pr1, Pr2, Rs, Rf, Rr,
    m1, m2, o1, o2, D, B, Br1, Br2, Zr1, Zr2, br, brg, U, Ur,
    ssem, rsem, lsem,
):
    ids = Ids()
    c = lax.axis_index("dp")
    f = lax.axis_index("fsdp")
    t = lax.axis_index("tensor")
    zl, y = f // 4, f % 4
    zh, x = t // 4, t % 4
    p = x % 2
    is_a = c == p
    is_b = c != p
    oc = 1 - c
    yR, yL, yO = (y + 1) % 4, (y + 3) % 4, (y + 2) % 4
    xR, xL, xO = (x + 1) % 4, (x + 3) % 4, (x + 2) % 4
    zR, zL, zO = (zh + 1) % 4, (zh + 3) % 4, (zh + 2) % 4
    zlO = 1 - zl
    fO = zlO * 4 + y

    def dev(core=c, zl_=zl, y_=y, zh_=zh, x_=x):
        return (core, zl_ * 4 + y_, zh_ * 4 + x_)

    def rc(src, dst, sid, rid, device):
        return pltpu.make_async_remote_copy(
            src_ref=src, dst_ref=dst, send_sem=ssem.at[sid], recv_sem=rsem.at[rid],
            device_id=device, device_id_type=MESH,
        )

    common, in_a, in_b = [], [], []

    def send(to, build):
        build().start()
        to.append(build)

    def wait_recv(dst, rid):
        rc(dst, dst, 0, rid, dev(core=oc)).wait_recv()

    def half(h):
        return pl.ds(pl.multiple_of(h * HALF, 16), HALF)

    qr_load = pltpu.make_async_copy(
        qr_hbm.at[pl.ds(pl.multiple_of(c * COLS, COLS), COLS)], Q.at[f], lsem.at[0])
    g_load = pltpu.make_async_copy(g_hbm.at[0], gv, lsem.at[1])
    ql_load = pltpu.make_async_copy(ql_hbm, QL, lsem.at[2])
    m1_load = pltpu.make_async_copy(m1_hbm, m1, lsem.at[3])
    m2_load = pltpu.make_async_copy(m2_hbm, m2, lsem.at[4])
    g_load.start()
    qr_load.start()
    ql_load.start()
    m1_load.start()
    m2_load.start()

    barrier = pltpu.get_barrier_semaphore()
    friends = [dev(core=oc), dev(x_=xR), dev(x_=xL)]
    for core in (c, oc):
        friends += [dev(core=core, y_=yR), dev(core=core, y_=yL), dev(core=core, zl_=zlO),
                    dev(core=core, zh_=zR), dev(core=core, zh_=zL)]
    for friend in friends:
        pl.semaphore_signal(barrier, inc=1, device_id=friend, device_id_type=MESH)
    pl.semaphore_wait(barrier, len(friends))

    g_load.wait()
    send(common, lambda: rc(gv.at[half(oc)], gx, ids.get("g"), ids.get("g"), dev(core=oc)))
    qr_load.wait()

    def qpart(slot, a):
        return Q.at[slot, pl.ds(a * 320, 320)]

    def qsend(name, slot, a, device):
        i = ids.get(name)
        send(common, lambda: rc(qpart(slot, a), qpart(slot, a), i, i, device))

    for a in range(2):
        qsend(("Qy+", "own", a), f, a, dev(y_=yR))
        qsend(("Qy-", "own", a), f, a, dev(y_=yL))

    wait_recv(gx, ids.get("g"))
    gs[...] = (gv[half(c), :].astype(F32) + gx[...].astype(F32)).astype(BF16)

    own = 2 * zh + x // 2

    def gpart(slot, h):
        return G.at[slot, half(h)]

    gz_p, gz_m = ids.get("Gz+", 2), ids.get("Gz-", 2)
    send(common, lambda: rc(gs, gpart(own, c), gz_p + c, gz_p + c, dev(core=p, zh_=zR)))
    send(common, lambda: rc(gs, gpart(own, c), gz_m + c, gz_m + c, dev(core=p, zh_=zL)))
    for a in range(2):
        qsend(("Qz", a), f, a, dev(zl_=zlO))

    gx_p, gx_m = ids.get("Gx+", 8), ids.get("Gx-", 8)
    zq = [zh, zL, zR, zO]
    gf_p, gf_m = ids.get("Gxf+", 4), ids.get("Gxf-", 4)
    id_gs, id_zf_p, id_zf_m = ids.get("Gs"), ids.get("Gzf+"), ids.get("Gzf-")

    def gslot(q, x_):
        return 2 * zq[q] + x_ // 2

    def a_spread(q, h, src=None):
        for base, x_ in ((gx_p, xR), (gx_m, xL)):
            send(in_a, lambda base=base, x_=x_: rc(
                gpart(gslot(q, x), h) if src is None else src, gpart(gslot(q, x), h),
                base + 2 * q + h, base + 2 * q + h, dev(x_=x_)))

    def qy_own_forward():
        i = ids.get(("Qy+", "own", 0))
        wait_recv(qpart(zl * 4 + yL, 0), i)
        qsend(("Qyf+", "own"), zl * 4 + yL, 0, dev(y_=yR))
        i = ids.get(("Qy-", "own", 1))
        wait_recv(qpart(zl * 4 + yR, 1), i)
        qsend(("Qyf-", "own"), zl * 4 + yR, 1, dev(y_=yL))

    def qz_spread():
        for a in range(2):
            wait_recv(qpart(fO, a), ids.get(("Qz", a)))
            qsend(("Qy+", "par", a), fO, a, dev(y_=yR))
            qsend(("Qy-", "par", a), fO, a, dev(y_=yL))

    def qy_par_forward():
        wait_recv(qpart(zlO * 4 + yL, 0), ids.get(("Qy+", "par", 0)))
        qsend(("Qyf+", "par"), zlO * 4 + yL, 0, dev(y_=yR))
        wait_recv(qpart(zlO * 4 + yR, 1), ids.get(("Qy-", "par", 1)))
        qsend(("Qyf-", "par"), zlO * 4 + yR, 1, dev(y_=yL))

    @pl.when(is_a)
    def _():
        a_spread(0, c, src=gs)
        G[own, half(c), :] = gs[...]
        wait_recv(gpart(own, oc), id_gs)
        a_spread(0, oc)
        wait_recv(gpart(gslot(1, x), 0), gz_p + 0)
        send(in_a, lambda: rc(gpart(gslot(1, x), 0), gpart(gslot(1, x), 0), id_zf_p, id_zf_p, dev(zh_=zR)))
        a_spread(1, 0)
        wait_recv(gpart(gslot(2, x), 1), gz_m + 1)
        send(in_a, lambda: rc(gpart(gslot(2, x), 1), gpart(gslot(2, x), 1), id_zf_m, id_zf_m, dev(zh_=zL)))
        a_spread(2, 1)

    def b_forward(q, h):
        if h == 0:
            wait_recv(gpart(gslot(q, xL), 0), gx_p + 2 * q)
            send(in_b, lambda: rc(gpart(gslot(q, xL), 0), gpart(gslot(q, xL), 0), gf_p + q, gf_p + q, dev(x_=xR)))
        else:
            wait_recv(gpart(gslot(q, xR), 1), gx_m + 2 * q + 1)
            send(in_b, lambda: rc(gpart(gslot(q, xR), 1), gpart(gslot(q, xR), 1), gf_m + q, gf_m + q, dev(x_=xL)))

    @pl.when(is_b)
    def _():
        send(in_b, lambda: rc(gs, gpart(own, c), id_gs, id_gs, dev(core=oc)))
        b_forward(0, 0)
        b_forward(0, 1)

    qy_own_forward()
    qz_spread()

    @pl.when(is_a)
    def _():
        wait_recv(gpart(gslot(1, x), 1), gz_p + 1)
        a_spread(1, 1)
        wait_recv(gpart(gslot(2, x), 0), gz_m + 0)
        a_spread(2, 0)
        wait_recv(gpart(gslot(3, x), 0), id_zf_p)
        a_spread(3, 0)
        wait_recv(gpart(gslot(3, x), 1), id_zf_m)
        a_spread(3, 1)

    @pl.when(is_b)
    def _():
        b_forward(1, 0)
        b_forward(2, 1)
        b_forward(1, 1)
        b_forward(2, 0)

    qy_par_forward()

    @pl.when(is_b)
    def _():
        b_forward(3, 0)
        b_forward(3, 1)
        for q in range(4):
            wait_recv(gpart(gslot(q, xL), 1), gx_p + 2 * q + 1)
            wait_recv(gpart(gslot(q, xR), 0), gx_m + 2 * q)

    @pl.when(is_a)
    def _():
        for q in range(4):
            wait_recv(gpart(gslot(q, xO), 0), gf_p + q)
            wait_recv(gpart(gslot(q, xO), 1), gf_m + q)

    wait_recv(qpart(zl * 4 + yL, 1), ids.get(("Qy+", "own", 1)))
    wait_recv(qpart(zl * 4 + yR, 0), ids.get(("Qy-", "own", 0)))
    wait_recv(qpart(zlO * 4 + yL, 1), ids.get(("Qy+", "par", 1)))
    wait_recv(qpart(zlO * 4 + yR, 0), ids.get(("Qy-", "par", 0)))
    wait_recv(qpart(zl * 4 + yO, 0), ids.get(("Qyf+", "own")))
    wait_recv(qpart(zl * 4 + yO, 1), ids.get(("Qyf-", "own")))

    T[...] = jnp.zeros_like(T)
    last = zlO * 4 + yO

    @pl.loop(0, 7)
    def _(i):
        slot = (last + 1 + i) % 8
        T[...] += jnp.dot(G[slot], Q[slot], preferred_element_type=F32)

    wait_recv(qpart(last, 0), ids.get(("Qyf+", "par")))
    wait_recv(qpart(last, 1), ids.get(("Qyf-", "par")))
    T[...] += jnp.dot(G[last], Q[last], preferred_element_type=F32)

    Ts[...] = T[...].astype(BF16)
    id_t = ids.get("T")
    send(common, lambda: rc(Ts, Tr, id_t, id_t, dev(core=oc)))
    ql_load.wait()
    wait_recv(Tr, id_t)
    Tb[...] = (T[...] + Tr[...].astype(F32)).astype(BF16)

    for group in range(2):
        start = pl.multiple_of(c * 1792 + group * 896, 128)
        Pb[pl.ds(group * 896, 896), :] = lax.dot_general(
            QL[:, pl.ds(start, 896)], Tb[...], (((0,), (0,)), ((), ())), preferred_element_type=F32
        ).astype(BF16)

    def pblock(zl_, y_):
        return Pb.at[pl.ds(pl.multiple_of((zl_ * 4 + y_) * HALF, 16), HALF)]

    def psend(name, src, dst, device):
        i = ids.get(name)
        send(common, lambda: rc(src, dst, i, i, device))

    psend("Py1+", pblock(0, yO), Pr1.at[0], dev(y_=yR))
    psend("Py1-", pblock(1, yO), Pr1.at[1], dev(y_=yL))
    psend("Py2+n", pblock(1, yR), Pr2.at[0, 1], dev(y_=yR))
    psend("Py2-n", pblock(0, yL), Pr2.at[1, 0], dev(y_=yL))

    def add_into(dst, *others):
        total = dst[...].astype(F32)
        for other in others:
            total = total + other[...].astype(F32)
        dst[...] = total.astype(dst.dtype)

    wait_recv(Pr1.at[0], ids.get("Py1+"))
    add_into(pblock(0, yR), Pr1.at[0])
    psend("Py2+a", pblock(0, yR), Pr2.at[0, 0], dev(y_=yR))
    wait_recv(Pr1.at[1], ids.get("Py1-"))
    add_into(pblock(1, yL), Pr1.at[1])
    psend("Py2-a", pblock(1, yL), Pr2.at[1, 1], dev(y_=yL))
    wait_recv(Pr2.at[0, 1], ids.get("Py2+n"))
    wait_recv(Pr2.at[1, 0], ids.get("Py2-n"))
    wait_recv(Pr2.at[0, 0], ids.get("Py2+a"))
    wait_recv(Pr2.at[1, 1], ids.get("Py2-a"))

    def block_total(zl_):
        return (pblock(zl_, y)[...].astype(F32) + Pr2[0, zl_].astype(F32)
                + Pr2[1, zl_].astype(F32))

    Rs[...] = block_total(zlO).astype(BF16)
    psend("Pz", Rs, Rr, dev(zl_=zlO))
    Rf[...] = block_total(zl)
    m1_load.wait()
    m2_load.wait()
    wait_recv(Rr, ids.get("Pz"))

    @pl.loop(0, HALF // 32)
    def _(i):
        r = pl.ds(pl.multiple_of(i * 32, 32), 32)
        rotated = Rf[r, :] + Rr[r, :].astype(F32)
        first = beta_first * m1[r, :] + (1.0 - beta_first) * rotated
        second = beta_second * m2[r, :] + (1.0 - beta_second) * rotated * rotated
        o1[r, :] = first
        o2[r, :] = second
        first_hat = first / (1.0 - beta_first**ADAM_STEP)
        second_hat = second / (1.0 - beta_second**ADAM_STEP)
        D[c, r, :] = (first_hat / (jnp.sqrt(second_hat) + epsilon)).astype(BF16)

    id_d = ids.get("D")
    send(common, lambda: rc(D.at[c], D.at[c], id_d, id_d, dev(core=oc)))
    o1_store = pltpu.make_async_copy(o1, o1_hbm, lsem.at[5])
    o2_store = pltpu.make_async_copy(o2, o2_hbm, lsem.at[6])
    o1_store.start()
    o2_store.start()

    def multiply(xi, h):
        @pl.loop(0, 4)
        def _(z):
            B[xi * 4 + z, half(h), :] = lax.dot_general(
                D[h], Q[2 * z + xi], (((1,), (1,)), ((), ())), preferred_element_type=F32
            ).astype(BF16)

    def chunk_half(k):
        return (c + k // 2) % 2

    def rows(k):
        return pl.ds(pl.multiple_of(chunk_half(k) * HALF + (k % 2) * SUB, 16), SUB)

    b1_p, b1_m = ids.get("Bx1+", 4), ids.get("Bx1-", 4)
    b2n_p, b2n_m = ids.get("Bx2+n", 4), ids.get("Bx2-n", 4)
    b2a_p, b2a_m = ids.get("Bx2+a", 4), ids.get("Bx2-a", 4)
    z1_p, z1_m = ids.get("Bz1+", 4), ids.get("Bz1-", 4)
    z2_p, z2_m = ids.get("Bz2+", 4), ids.get("Bz2-", 4)
    fs_s, fz_s, fyp_s, fym_s = ids.get("Fs", 4), ids.get("Fz", 4), ids.get("Fy+", 4), ids.get("Fy-", 4)
    fpp, fpm = ids.get("Fyp+", 2), ids.get("Fyp-", 2)
    ffo_p, ffo_m, ffp_p, ffp_m = ids.get("Ff+o"), ids.get("Ff-o"), ids.get("Ff+p"), ids.get("Ff-p")

    def brpart(f_, s):
        return brg.at[pl.ds(pl.multiple_of(f_ * HALF + s * SUB, 16), SUB)]

    def f_spread(to, s):
        wait_recv(brpart(fO, s), fz_s + s)
        send(to, lambda: rc(brpart(fO, s), brpart(fO, s), fpp + s, fpp + s, dev(y_=yR)))
        send(to, lambda: rc(brpart(fO, s), brpart(fO, s), fpm + s, fpm + s, dev(y_=yL)))

    def f_forward_own(to, s):
        if s == 0:
            wait_recv(brpart(zl * 4 + yL, 0), fyp_s + 0)
            send(to, lambda: rc(brpart(zl * 4 + yL, 0), brpart(zl * 4 + yL, 0), ffo_p, ffo_p, dev(y_=yR)))
        else:
            wait_recv(brpart(zl * 4 + yR, 1), fym_s + 1)
            send(to, lambda: rc(brpart(zl * 4 + yR, 1), brpart(zl * 4 + yR, 1), ffo_m, ffo_m, dev(y_=yL)))

    def f_forward_partner(to, s):
        if s == 0:
            wait_recv(brpart(zlO * 4 + yL, 0), fpp + 0)
            send(to, lambda: rc(brpart(zlO * 4 + yL, 0), brpart(zlO * 4 + yL, 0), ffp_p, ffp_p, dev(y_=yR)))
        else:
            wait_recv(brpart(zlO * 4 + yR, 1), fpm + 1)
            send(to, lambda: rc(brpart(zlO * 4 + yR, 1), brpart(zlO * 4 + yR, 1), ffp_m, ffp_m, dev(y_=yL)))

    def add_blocks(first, count, r, terms):
        @pl.loop(0, count)
        def _(i):
            dst = B.at[first + i, r]
            total = dst[...].astype(F32)
            for term in terms(i):
                total = total + term[...].astype(F32)
            dst[...] = total.astype(BF16)

    @pl.when(is_a)
    def _():
        xi_own, xi_opp = x // 2, 1 - x // 2

        def opp_sends(k):
            def pair(first, base, x_):
                send(in_a, lambda: rc(B.at[pl.ds((1 - x // 2) * 4 + first, 2), rows(k)],
                                      Br1.at[pl.ds(first, 2), rows(k)], base + k, base + k, dev(x_=x_)))
            pair(0, b1_p, xR)
            pair(2, b1_m, xL)

        multiply(xi_opp, c)
        opp_sends(0)
        opp_sends(1)
        multiply(xi_own, c)
        wait_recv(D.at[oc], id_d)
        multiply(xi_opp, oc)
        opp_sends(2)
        opp_sends(3)
        multiply(xi_own, oc)

        def block(z_, k):
            return B.at[(x // 2) * 4 + z_, rows(k)]

        def reduce_chunk(k):
            r = rows(k)
            wait_recv(Br2.at[0, pl.ds(2, 2), r], b2n_p + k)
            wait_recv(Br2.at[1, pl.ds(0, 2), r], b2n_m + k)
            wait_recv(Br2.at[0, pl.ds(0, 2), r], b2a_p + k)
            wait_recv(Br2.at[1, pl.ds(2, 2), r], b2a_m + k)
            add_blocks(xi_own * 4, 4, r, lambda i: (Br2.at[0, i, r], Br2.at[1, i, r]))
            if k % 2 == 0:
                send(in_a, lambda: rc(block(zO, k), Zr1.at[rows(k)], z1_p + k, z1_p + k, dev(zh_=zR)))
                send(in_a, lambda: rc(block(zL, k), Zr2.at[1, rows(k)], z2_m + k, z2_m + k, dev(zh_=zL)))
                wait_recv(Zr1.at[r], z1_p + k)
                add_into(block(zR, k), Zr1.at[r])
                send(in_a, lambda: rc(block(zR, k), Zr2.at[0, rows(k)], z2_p + k, z2_p + k, dev(zh_=zR)))
            else:
                send(in_a, lambda: rc(block(zO, k), Zr1.at[rows(k)], z1_m + k, z1_m + k, dev(zh_=zL)))
                send(in_a, lambda: rc(block(zR, k), Zr2.at[0, rows(k)], z2_p + k, z2_p + k, dev(zh_=zR)))
                wait_recv(Zr1.at[r], z1_m + k)
                add_into(block(zL, k), Zr1.at[r])
                send(in_a, lambda: rc(block(zL, k), Zr2.at[1, rows(k)], z2_m + k, z2_m + k, dev(zh_=zL)))
            wait_recv(Zr2.at[0, r], z2_p + k)
            wait_recv(Zr2.at[1, r], z2_m + k)
            total = (block(zh, k)[...].astype(F32) + Zr2[0, r, :].astype(F32)
                     + Zr2[1, r, :].astype(F32)).astype(BF16)
            br[r, :] = total
            s = k % 2
            core = chunk_half(k)
            send(in_a, lambda: rc(br.at[rows(k)], brpart(f, s), fz_s + k, fz_s + s, dev(core=chunk_half(k), zl_=zlO)))
            send(in_a, lambda: rc(br.at[rows(k)], brpart(f, s), fyp_s + k, fyp_s + s, dev(core=chunk_half(k), y_=yR)))
            send(in_a, lambda: rc(br.at[rows(k)], brpart(f, s), fym_s + k, fym_s + s, dev(core=chunk_half(k), y_=yL)))
            if k < 2:
                brpart(f, s)[...] = total
            else:
                send(in_a, lambda: rc(br.at[rows(k)], brpart(f, s), fs_s + k, fs_s + s, dev(core=oc)))

        reduce_chunk(0)
        reduce_chunk(1)
        f_spread(in_a, 0)
        f_forward_own(in_a, 0)
        reduce_chunk(2)
        f_spread(in_a, 1)
        f_forward_own(in_a, 1)
        f_forward_partner(in_a, 0)
        reduce_chunk(3)
        f_forward_partner(in_a, 1)

    @pl.when(is_b)
    def _():
        xi_r, xi_l = xR // 2, xL // 2

        def x_send(first, xi_of, d, base, k, x_):
            send(in_b, lambda: rc(B.at[pl.ds(xi_of // 2 * 4 + first, 2), rows(k)],
                                  Br2.at[d, pl.ds(first, 2), rows(k)], base + k, base + k, dev(x_=x_)))

        def plain_sends(k):
            x_send(2, xR, 0, b2n_p, k, xR)
            x_send(0, xL, 1, b2n_m, k, xL)

        def sum_sends(k):
            r = rows(k)
            wait_recv(Br1.at[pl.ds(0, 2), r], b1_p + k)
            add_blocks(xi_r * 4, 2, r, lambda i: (Br1.at[i, r],))
            x_send(0, xR, 0, b2a_p, k, xR)
            wait_recv(Br1.at[pl.ds(2, 2), r], b1_m + k)
            add_blocks(xi_l * 4 + 2, 2, r, lambda i: (Br1.at[2 + i, r],))
            x_send(2, xL, 1, b2a_m, k, xL)

        multiply(0, c)
        multiply(1, c)
        plain_sends(0)
        plain_sends(1)
        wait_recv(D.at[oc], id_d)
        multiply(0, oc)
        multiply(1, oc)
        sum_sends(0)
        sum_sends(1)
        plain_sends(2)
        plain_sends(3)
        sum_sends(2)
        sum_sends(3)
        for s in range(2):
            f_spread(in_b, s)
            f_forward_own(in_b, s)
        for s in range(2):
            f_forward_partner(in_b, s)
        for s in range(2):
            wait_recv(brpart(f, s), fs_s + s)

    wait_recv(brpart(zl * 4 + yL, 1), fyp_s + 1)
    wait_recv(brpart(zl * 4 + yR, 0), fym_s + 0)
    wait_recv(brpart(zlO * 4 + yL, 1), fpp + 1)
    wait_recv(brpart(zlO * 4 + yR, 0), fpm + 0)
    wait_recv(brpart(zl * 4 + yO, 0), ffo_p)
    wait_recv(brpart(zl * 4 + yO, 1), ffo_m)
    wait_recv(brpart(zlO * 4 + yO, 0), ffp_p)
    wait_recv(brpart(zlO * 4 + yO, 1), ffp_m)

    start = pl.multiple_of(c * 1792, 128)
    U[...] = jnp.dot(QL[:, pl.ds(start, 896)], brg[pl.ds(0, 896), :], preferred_element_type=F32)
    start = pl.multiple_of(c * 1792 + 896, 128)
    U[...] += jnp.dot(QL[:, pl.ds(start, 896)], brg[pl.ds(896, 896), :], preferred_element_type=F32)
    id_u = ids.get("U")
    send(common, lambda: rc(U, Ur, id_u, id_u, dev(core=oc)))
    wait_recv(Ur, id_u)
    Ur[...] = Ur[...] + U[...]
    up_store = pltpu.make_async_copy(Ur, up_hbm, lsem.at[7])
    up_store.start()

    for build in common:
        build().wait_send()

    @pl.when(is_a)
    def _():
        for build in in_a:
            build().wait_send()

    @pl.when(is_b)
    def _():
        for build in in_b:
            build().wait_send()

    o1_store.wait()
    o2_store.wait()
    up_store.wait()
    assert ids.count <= SEMS, ids.count


SEMS = 160


def per_device(replica_grads, basis_left, basis_right, first_moment, second_moment):
    any_space = pl.BlockSpec(memory_space=pl.ANY)
    v = pltpu.VMEM
    scratch = [
        v((ROWS, COLS), BF16),
        v((HALF, COLS), BF16),
        v((HALF, COLS), BF16),
        v((8, ROWS, COLS), BF16),
        v((8, COLS, COLS), BF16),
        v((ROWS, 3584), BF16),
        v((ROWS, COLS), F32),
        v((ROWS, COLS), BF16),
        v((ROWS, COLS), BF16),
        v((ROWS, COLS), BF16),
        v((8 * HALF, COLS), BF16),
        v((2, HALF, COLS), BF16),
        v((2, 2, HALF, COLS), BF16),
        v((HALF, COLS), BF16),
        v((HALF, COLS), F32),
        v((HALF, COLS), BF16),
        v((HALF, COLS), F32),
        v((HALF, COLS), F32),
        v((HALF, COLS), F32),
        v((HALF, COLS), F32),
        v((2, HALF, COLS), BF16),
        v((8, ROWS, COLS), BF16),
        v((4, ROWS, COLS), BF16),
        v((2, 4, ROWS, COLS), BF16),
        v((ROWS, COLS), BF16),
        v((2, ROWS, COLS), BF16),
        v((ROWS, COLS), BF16),
        v((8 * HALF, COLS), BF16),
        v((ROWS, COLS), F32),
        v((ROWS, COLS), F32),
        pltpu.SemaphoreType.DMA((SEMS,)),
        pltpu.SemaphoreType.DMA((SEMS,)),
        pltpu.SemaphoreType.DMA((8,)),
    ]
    return pl.pallas_call(
        kernel,
        out_shape=(
            jax.ShapeDtypeStruct((HALF, COLS), F32),
            jax.ShapeDtypeStruct((HALF, COLS), F32),
            jax.ShapeDtypeStruct((ROWS, COLS), F32),
        ),
        in_specs=[any_space] * 5,
        out_specs=(any_space,) * 3,
        scratch_shapes=scratch,
        compiler_params=pltpu.CompilerParams(
            collective_id=0, has_side_effects=True, vmem_limit_bytes=60 * 2**20
        ),
        cost_estimate=pl.CostEstimate(
            flops=9 * 10**9, bytes_accessed=10 * 2**20, transcendentals=HALF * COLS
        ),
        name="soap_step",
    )(replica_grads, basis_left, basis_right, first_moment, second_moment)


def solution(mesh):
    placed = (
        P("dp", "fsdp", "tensor"),
        P("fsdp", None),
        P("fsdp", "tensor"),
        P(("dp", "fsdp"), "tensor"),
        P(("dp", "fsdp"), "tensor"),
    )
    return jax.shard_map(
        per_device,
        mesh=mesh,
        in_specs=placed,
        out_specs=(P(("dp", "fsdp"), "tensor"), P(("dp", "fsdp"), "tensor"), P("fsdp", "tensor")),
        check_vma=False,
    )
```

```python
import functools

import jax
import jax.numpy as jnp
from jax import lax
from jax.experimental import pallas as pl
from jax.experimental.pallas import tpu as pltpu
from jax.sharding import PartitionSpec as P

MESH = pl.DeviceIdType.MESH
F32 = jnp.float32
BF16 = jnp.bfloat16

ADAM_STEP = 10
beta_first = 0.9
beta_second = 0.95
epsilon = 1e-08

ROWS = 448
HALF = 224
COLS = 640
SUB = 112
YF = 384
WIDTHS = (128, 128, 128, 128, 128)


class Ids:
    def __init__(self):
        self.table = {}
        self.count = 0

    def get(self, name, width=1):
        if name not in self.table:
            self.table[name] = self.count
            self.count += width
        return self.table[name]


def kernel(
    g_hbm, ql_hbm, qr_hbm, m1_hbm, m2_hbm,
    rot_hbm, u_hbm,
    gv, gx, gs, G, Q, QL, QT, T, Ts, Tr, Tb, P0, P1, Pr1, Pr2, Rs, Rf, Rr, Zp, Sy1, Sy2,
    m1, m2, D, Bs, Br1s, Br2s, Zrs, brs, brgs, Us,
    ssem, rsem, lsem,
):
    ids = Ids()
    c = lax.axis_index("dp")
    f = lax.axis_index("fsdp")
    t = lax.axis_index("tensor")
    zl, y = f // 4, f % 4
    zh, x = t // 4, t % 4
    p = x % 2
    is_a = c == p
    is_b = c != p
    oc = 1 - c
    yR, yL, yO = (y + 1) % 4, (y + 3) % 4, (y + 2) % 4
    xR, xL, xO = (x + 1) % 4, (x + 3) % 4, (x + 2) % 4
    zR, zL, zO = (zh + 1) % 4, (zh + 3) % 4, (zh + 2) % 4
    zlO = 1 - zl
    fO = zlO * 4 + y

    def dev(core=c, zl_=zl, y_=y, zh_=zh, x_=x):
        return (core, zl_ * 4 + y_, zh_ * 4 + x_)

    def rc(src, dst, sid, rid, device):
        return pltpu.make_async_remote_copy(
            src_ref=src, dst_ref=dst, send_sem=ssem.at[sid], recv_sem=rsem.at[rid],
            device_id=device, device_id_type=MESH,
        )

    common, in_a, in_b = [], [], []

    def send(to, build):
        build().start()
        to.append(build)

    def wait_recv(dst, rid):
        rc(dst, dst, 0, rid, dev(core=oc)).wait_recv()

    def half(h):
        return pl.ds(pl.multiple_of(h * HALF, 16), HALF)

    qr_load = pltpu.make_async_copy(
        qr_hbm.at[pl.ds(pl.multiple_of(c * COLS, COLS), COLS)], Q.at[f], lsem.at[0])
    g_load = pltpu.make_async_copy(g_hbm.at[0], gv, lsem.at[1])
    ql_load = pltpu.make_async_copy(ql_hbm, QL, lsem.at[2])
    m1_load = pltpu.make_async_copy(m1_hbm, m1, lsem.at[3])
    m2_load = pltpu.make_async_copy(m2_hbm, m2, lsem.at[4])
    g_load.start()
    qr_load.start()
    ql_load.start()
    m1_load.start()
    m2_load.start()

    barrier = pltpu.get_barrier_semaphore()
    friends = [dev(core=oc), dev(x_=xR), dev(x_=xL)]
    for core in (c, oc):
        friends += [dev(core=core, y_=yR), dev(core=core, y_=yL), dev(core=core, zl_=zlO),
                    dev(core=core, zh_=zR), dev(core=core, zh_=zL)]
    for friend in friends:
        pl.semaphore_signal(barrier, inc=1, device_id=friend, device_id_type=MESH)
    pl.semaphore_wait(barrier, len(friends))

    g_load.wait()
    send(common, lambda: rc(gv.at[half(oc)], gx, ids.get("g"), ids.get("g"), dev(core=oc)))
    qr_load.wait()

    def qpart(slot, a):
        return Q.at[slot, pl.ds(a * 320, 320)]

    def qsend(name, slot, a, device):
        i = ids.get(name)
        send(common, lambda: rc(qpart(slot, a), qpart(slot, a), i, i, device))

    def qy_own(a):
        qsend(("Qy+", "own", a), f, a, dev(y_=yR))
        qsend(("Qy-", "own", a), f, a, dev(y_=yL))

    def qz_send(a):
        qsend(("Qz", a), f, a, dev(zl_=zlO))

    qy_own(0)
    qz_send(0)
    qy_own(1)

    wait_recv(gx, ids.get("g"))
    gs[...] = (gv[half(c), :].astype(F32) + gx[...].astype(F32)).astype(BF16)

    own = 2 * zh + x // 2

    def gpart(slot, h):
        return G.at[slot, half(h)]

    gz_p, gz_m = ids.get("Gz+", 2), ids.get("Gz-", 2)
    send(common, lambda: rc(gs, gpart(own, c), gz_p + c, gz_p + c, dev(core=p, zh_=zR)))
    send(common, lambda: rc(gs, gpart(own, c), gz_m + c, gz_m + c, dev(core=p, zh_=zL)))
    gx_p, gx_m = ids.get("Gx+", 8), ids.get("Gx-", 8)
    zq = [zh, zL, zR, zO]
    gf_p, gf_m = ids.get("Gxf+", 4), ids.get("Gxf-", 4)
    id_gs, id_zf_p, id_zf_m = ids.get("Gs"), ids.get("Gzf+"), ids.get("Gzf-")

    def gslot(q, x_):
        return 2 * zq[q] + x_ // 2

    def a_spread(q, h, src=None):
        for base, x_ in ((gx_p, xR), (gx_m, xL)):
            send(in_a, lambda base=base, x_=x_: rc(
                gpart(gslot(q, x), h) if src is None else src, gpart(gslot(q, x), h),
                base + 2 * q + h, base + 2 * q + h, dev(x_=x_)))

    def qy_own_forward():
        i = ids.get(("Qy+", "own", 0))
        wait_recv(qpart(zl * 4 + yL, 0), i)
        qsend(("Qyf+", "own"), zl * 4 + yL, 0, dev(y_=yR))
        i = ids.get(("Qy-", "own", 1))
        wait_recv(qpart(zl * 4 + yR, 1), i)
        qsend(("Qyf-", "own"), zl * 4 + yR, 1, dev(y_=yL))

    def qz_spread(a):
        wait_recv(qpart(fO, a), ids.get(("Qz", a)))
        qsend(("Qy+", "par", a), fO, a, dev(y_=yR))
        qsend(("Qy-", "par", a), fO, a, dev(y_=yL))

    def transpose_left(group):
        start = pl.multiple_of(c * 1792 + group * 896, 128)
        QT[pl.ds(group * 896, 896), :] = QL[:, pl.ds(start, 896)].T

    def qy_par_forward():
        wait_recv(qpart(zlO * 4 + yL, 0), ids.get(("Qy+", "par", 0)))
        qsend(("Qyf+", "par"), zlO * 4 + yL, 0, dev(y_=yR))
        wait_recv(qpart(zlO * 4 + yR, 1), ids.get(("Qy-", "par", 1)))
        qsend(("Qyf-", "par"), zlO * 4 + yR, 1, dev(y_=yL))

    def b_forward(q, h):
        if h == 0:
            wait_recv(gpart(gslot(q, xL), 0), gx_p + 2 * q)
            send(in_b, lambda: rc(gpart(gslot(q, xL), 0), gpart(gslot(q, xL), 0), gf_p + q, gf_p + q, dev(x_=xR)))
        else:
            wait_recv(gpart(gslot(q, xR), 1), gx_m + 2 * q + 1)
            send(in_b, lambda: rc(gpart(gslot(q, xR), 1), gpart(gslot(q, xR), 1), gf_m + q, gf_m + q, dev(x_=xL)))

    @pl.when(is_a)
    def _():
        a_spread(0, c, src=gs)
        G[own, half(c), :] = gs[...]
        wait_recv(gpart(own, oc), id_gs)
        a_spread(0, oc)
        wait_recv(gpart(gslot(1, x), 0), gz_p + 0)
        send(in_a, lambda: rc(gpart(gslot(1, x), 0), gpart(gslot(1, x), 0), id_zf_p, id_zf_p, dev(zh_=zR)))
        a_spread(1, 0)
        wait_recv(gpart(gslot(2, x), 1), gz_m + 1)
        send(in_a, lambda: rc(gpart(gslot(2, x), 1), gpart(gslot(2, x), 1), id_zf_m, id_zf_m, dev(zh_=zL)))
        a_spread(2, 1)

    @pl.when(is_b)
    def _():
        send(in_b, lambda: rc(gs, gpart(own, c), id_gs, id_gs, dev(core=oc)))
        b_forward(0, 0)
        b_forward(0, 1)

    qz_send(1)
    ql_load.wait()
    transpose_left(0)

    @pl.when(is_a)
    def _():
        wait_recv(gpart(gslot(1, x), 1), gz_p + 1)
        a_spread(1, 1)
        wait_recv(gpart(gslot(2, x), 0), gz_m + 0)
        a_spread(2, 0)

    qy_own_forward()

    @pl.when(is_a)
    def _():
        wait_recv(gpart(gslot(3, x), 0), id_zf_p)
        a_spread(3, 0)
        wait_recv(gpart(gslot(3, x), 1), id_zf_m)
        a_spread(3, 1)

    @pl.when(is_b)
    def _():
        b_forward(1, 0)
        b_forward(2, 1)

    qz_spread(0)

    @pl.when(is_b)
    def _():
        b_forward(1, 1)
        b_forward(2, 0)

    qz_spread(1)
    transpose_left(1)

    @pl.when(is_b)
    def _():
        b_forward(3, 0)
        b_forward(3, 1)

    qy_par_forward()

    @pl.when(is_b)
    def _():
        for q in range(4):
            wait_recv(gpart(gslot(q, xL), 1), gx_p + 2 * q + 1)
            wait_recv(gpart(gslot(q, xR), 0), gx_m + 2 * q)

    @pl.when(is_a)
    def _():
        for q in range(4):
            wait_recv(gpart(gslot(q, xO), 0), gf_p + q)
            wait_recv(gpart(gslot(q, xO), 1), gf_m + q)

    wait_recv(qpart(zl * 4 + yL, 1), ids.get(("Qy+", "own", 1)))
    wait_recv(qpart(zl * 4 + yR, 0), ids.get(("Qy-", "own", 0)))
    wait_recv(qpart(zlO * 4 + yL, 1), ids.get(("Qy+", "par", 1)))
    wait_recv(qpart(zlO * 4 + yR, 0), ids.get(("Qy-", "par", 0)))
    wait_recv(qpart(zl * 4 + yO, 0), ids.get(("Qyf+", "own")))
    wait_recv(qpart(zl * 4 + yO, 1), ids.get(("Qyf-", "own")))

    T[...] = jnp.zeros_like(T)
    last = zlO * 4 + yO

    @pl.loop(0, 7)
    def _(i):
        slot = (last + 1 + i) % 8
        T[...] += jnp.dot(G[slot], Q[slot], preferred_element_type=F32)

    wait_recv(qpart(last, 0), ids.get(("Qyf+", "par")))
    wait_recv(qpart(last, 1), ids.get(("Qyf-", "par")))
    T[...] += jnp.dot(G[last], Q[last], preferred_element_type=F32)

    Ts[...] = T[...].astype(BF16)
    id_t = ids.get("T")
    send(common, lambda: rc(Ts, Tr, id_t, id_t, dev(core=oc)))
    wait_recv(Tr, id_t)
    Tb[...] = (T[...] + Tr[...].astype(F32)).astype(BF16)

    def left(buf, group, lo, width):
        r = pl.ds(pl.multiple_of(group * 896, 128), 896)
        buf[r, :] = jnp.dot(
            QT[r, :], Tb[:, lo:lo + width], preferred_element_type=F32).astype(BF16)

    def pblock(buf, zl_, y_):
        return buf.at[pl.ds(pl.multiple_of((zl_ * 4 + y_) * HALF, 16), HALF)]

    def spart(y_, s):
        return P1.at[pl.ds(pl.multiple_of((zl * 4 + y_) * HALF + s * SUB, 16), SUB)]

    def half_of(buf, s):
        return buf.at[pl.ds(s * SUB, SUB)]

    def psend(name, src, dst, device):
        i = ids.get(name)
        send(common, lambda: rc(src, dst, i, i, device))

    def add_into(dst, *others):
        total = dst[...].astype(F32)
        for other in others:
            total = total + other[...].astype(F32)
        dst[...] = total.astype(dst.dtype)

    left(P1, zlO, YF, COLS - YF)
    for name, y_ in (("O", yO), ("R", yR), ("L", yL), ("S", y)):
        psend(("Pz1", name), pblock(P1, zlO, y_), Zp.at[y_], dev(zl_=zlO))
    left(P0, 0, 0, YF)
    psend("Py1+", pblock(P0, 0, yO), Pr1.at[0], dev(y_=yR))
    psend("Py2-n", pblock(P0, 0, yL), Pr2.at[1, 0], dev(y_=yL))
    left(P0, 1, 0, YF)
    psend("Py1-", pblock(P0, 1, yO), Pr1.at[1], dev(y_=yL))
    psend("Py2+n", pblock(P0, 1, yR), Pr2.at[0, 1], dev(y_=yR))
    left(P1, zl, YF, COLS - YF)

    def z_add(name, y_):
        wait_recv(Zp.at[y_], ids.get(("Pz1", name)))
        add_into(pblock(P1, zl, y_), Zp.at[y_])

    z_add("O", yO)
    psend("Sy1+", spart(yO, 0), Sy1.at[0], dev(y_=yR))
    psend("Sy1-", spart(yO, 1), Sy1.at[1], dev(y_=yL))
    wait_recv(Pr1.at[0], ids.get("Py1+"))
    add_into(pblock(P0, 0, yR), Pr1.at[0])
    psend("Py2+a", pblock(P0, 0, yR), Pr2.at[0, 0], dev(y_=yR))
    wait_recv(Pr1.at[1], ids.get("Py1-"))
    add_into(pblock(P0, 1, yL), Pr1.at[1])
    psend("Py2-a", pblock(P0, 1, yL), Pr2.at[1, 1], dev(y_=yL))
    z_add("R", yR)
    psend("Sy2+n", spart(yR, 1), half_of(Sy2.at[0], 1), dev(y_=yR))
    wait_recv(Sy1.at[0], ids.get("Sy1+"))
    add_into(spart(yR, 0), Sy1.at[0])
    psend("Sy2+a", spart(yR, 0), half_of(Sy2.at[0], 0), dev(y_=yR))
    z_add("L", yL)
    psend("Sy2-n", spart(yL, 0), half_of(Sy2.at[1], 0), dev(y_=yL))
    wait_recv(Sy1.at[1], ids.get("Sy1-"))
    add_into(spart(yL, 1), Sy1.at[1])
    psend("Sy2-a", spart(yL, 1), half_of(Sy2.at[1], 1), dev(y_=yL))
    wait_recv(Pr2.at[0, 1], ids.get("Py2+n"))
    wait_recv(Pr2.at[1, 0], ids.get("Py2-n"))
    wait_recv(Pr2.at[0, 0], ids.get("Py2+a"))
    wait_recv(Pr2.at[1, 1], ids.get("Py2-a"))

    def block_total(zl_):
        return (pblock(P0, zl_, y)[...].astype(F32) + Pr2[0, zl_].astype(F32)
                + Pr2[1, zl_].astype(F32))

    Rs[...] = block_total(zlO).astype(BF16)
    psend("Pz", Rs, Rr, dev(zl_=zlO))
    Rf[:, 0:YF] = block_total(zl)
    wait_recv(Zp.at[y], ids.get(("Pz1", "S")))
    total = pblock(P1, zl, y)[...].astype(F32) + Zp[y].astype(F32)
    wait_recv(half_of(Sy2.at[0], 0), ids.get("Sy2+a"))
    wait_recv(half_of(Sy2.at[0], 1), ids.get("Sy2+n"))
    wait_recv(half_of(Sy2.at[1], 0), ids.get("Sy2-n"))
    wait_recv(half_of(Sy2.at[1], 1), ids.get("Sy2-a"))
    Rf[:, YF:COLS] = total + Sy2[0].astype(F32) + Sy2[1].astype(F32)
    m1_load.wait()
    m2_load.wait()
    wait_recv(Rr, ids.get("Pz"))

    def adam(r, lo, hi, rotated):
        Rf[r, lo:hi] = rotated
        first = beta_first * m1[r, lo:hi] + (1.0 - beta_first) * rotated
        second = beta_second * m2[r, lo:hi] + (1.0 - beta_second) * rotated * rotated
        first_hat = first / (1.0 - beta_first**ADAM_STEP)
        second_hat = second / (1.0 - beta_second**ADAM_STEP)
        where = pl.ds(pl.multiple_of(c * HALF + r.start, 16), 32)
        D[where, lo:hi] = (first_hat / (jnp.sqrt(second_hat) + epsilon)).astype(BF16)

    @pl.loop(0, HALF // 32)
    def _(i):
        r = pl.ds(pl.multiple_of(i * 32, 32), 32)
        adam(r, 0, YF, Rf[r, 0:YF] + Rr[r, :].astype(F32))
        adam(r, YF, COLS, Rf[r, YF:COLS])

    id_d = ids.get("D")
    send(common, lambda: rc(D.at[half(c)], D.at[half(c)], id_d, id_d, dev(core=oc)))
    rot_store = pltpu.make_async_copy(Rf, rot_hbm, lsem.at[5])
    rot_store.start()
    wait_recv(D.at[half(oc)], id_d)

    chunks = range(len(WIDTHS))
    lows = [sum(WIDTHS[:k]) for k in chunks]
    n = len(WIDTHS)

    def multiply(k, xi):
        @pl.loop(0, 4)
        def _(z):
            Bs[k][xi * 4 + z] = lax.dot_general(
                D[...], Q[2 * z + xi, pl.ds(lows[k], WIDTHS[k])],
                (((1,), (1,)), ((), ())), preferred_element_type=F32
            ).astype(BF16)

    b1_p, b1_m = ids.get("Bx1+", n), ids.get("Bx1-", n)
    b2n_p, b2n_m = ids.get("Bx2+n", n), ids.get("Bx2-n", n)
    b2a_p, b2a_m = ids.get("Bx2+a", n), ids.get("Bx2-a", n)
    z_p, z_m, z_o = ids.get("Bz+", n), ids.get("Bz-", n), ids.get("Bzo", n)
    fs, fz = ids.get("Fs", n), ids.get("Fz", 2 * n)
    fy = [ids.get(("Fy", d), 2 * n) for d in range(3)]
    fp = [ids.get(("Fp", d), n) for d in range(3)]
    id_u = ids.get("U", n)

    ys = (yR, yL, yO)
    sources = (yL, yR, yO)

    def brrows(k, f_):
        return brgs[k].at[pl.ds(pl.multiple_of(f_ * HALF, 16), HALF)]

    def f_spread(to, k):
        wait_recv(brrows(k, fO), fz + k)
        for d in range(3):
            send(to, lambda d=d: rc(brrows(k, fO), brrows(k, fO), fp[d] + k, fp[d] + k, dev(y_=ys[d])))

    def final(k):
        for d in range(3):
            wait_recv(brrows(k, zl * 4 + sources[d]), fy[d] + k)
            wait_recv(brrows(k, zlO * 4 + sources[d]), fp[d] + k)
        start = pl.multiple_of(c * 1792, 128)
        Us[k][c] = jnp.dot(QL[:, pl.ds(start, 1792)], brgs[k][...], preferred_element_type=F32)

    def final_send(to, k):
        send(to, lambda: rc(Us[k].at[c], Us[k].at[c], id_u + k, id_u + k, dev(core=oc)))

    def u_store(k, core):
        return pltpu.make_async_copy(
            Us[k].at[core], u_hbm.at[core, :, pl.ds(lows[k], WIDTHS[k])], lsem.at[6 + 2 * k + core])

    def finish(k):
        u_store(k, c).start()
        wait_recv(Us[k].at[oc], id_u + k)
        u_store(k, oc).start()

    def add_blocks(buf, first, count, terms):
        @pl.loop(0, count)
        def _(i):
            dst = buf.at[first + i]
            total = dst[...].astype(F32)
            for term in terms(i):
                total = total + term[...].astype(F32)
            dst[...] = total.astype(BF16)

    @pl.when(is_a)
    def _():
        xi_own, xi_opp = x // 2, 1 - x // 2

        def opp_sends(k):
            send(in_a, lambda: rc(Bs[k].at[pl.ds((1 - x // 2) * 4, 2)], Br1s[k].at[pl.ds(0, 2)],
                                  b1_p + k, b1_p + k, dev(x_=xR)))
            send(in_a, lambda: rc(Bs[k].at[pl.ds((1 - x // 2) * 4 + 2, 2)], Br1s[k].at[pl.ds(2, 2)],
                                  b1_m + k, b1_m + k, dev(x_=xL)))

        def block(k, z_):
            return Bs[k].at[(x // 2) * 4 + z_]

        def x_total(k):
            wait_recv(Br2s[k].at[0, pl.ds(2, 2)], b2n_p + k)
            wait_recv(Br2s[k].at[1, pl.ds(0, 2)], b2n_m + k)
            wait_recv(Br2s[k].at[0, pl.ds(0, 2)], b2a_p + k)
            wait_recv(Br2s[k].at[1, pl.ds(2, 2)], b2a_m + k)
            add_blocks(Bs[k], xi_own * 4, 4, lambda i: (Br2s[k].at[0, i], Br2s[k].at[1, i]))
            send(in_a, lambda: rc(block(k, zR), Zrs[k].at[0], z_p + k, z_p + k, dev(zh_=zR)))
            send(in_a, lambda: rc(block(k, zL), Zrs[k].at[1], z_m + k, z_m + k, dev(zh_=zL)))
            send(in_a, lambda: rc(block(k, zO), Zrs[k].at[2], z_o + k, z_o + k, dev(zh_=zO)))

        def z_total(k):
            wait_recv(Zrs[k].at[0], z_p + k)
            wait_recv(Zrs[k].at[1], z_m + k)
            wait_recv(Zrs[k].at[2], z_o + k)
            brs[k][...] = (Bs[k][(x // 2) * 4 + zh].astype(F32) + Zrs[k][0].astype(F32)
                           + Zrs[k][1].astype(F32) + Zrs[k][2].astype(F32)).astype(BF16)
            for other in range(2):
                def src(other=other):
                    return brs[k].at[half(oc if other else c)]

                def to(other=other, **moved):
                    return dev(core=oc if other else c, **moved)

                send(in_a, lambda src=src, to=to, other=other: rc(
                    src(), brrows(k, f), fz + k + n * other, fz + k, to(zl_=zlO)))
                for d in range(3):
                    send(in_a, lambda src=src, to=to, other=other, d=d: rc(
                        src(), brrows(k, f), fy[d] + k + n * other, fy[d] + k, to(y_=ys[d])))
            send(in_a, lambda: rc(brs[k].at[half(oc)], brrows(k, f), fs + k, fs + k, dev(core=oc)))
            brrows(k, f)[...] = brs[k][half(c), :]

        def start_chunk(k):
            multiply(k, xi_opp)
            opp_sends(k)
            multiply(k, xi_own)

        start_chunk(0)
        start_chunk(1)
        for k in range(n + 4):
            if k < n:
                x_total(k)
            if k + 2 < n:
                start_chunk(k + 2)
            if 0 <= k - 1 < n:
                z_total(k - 1)
            if 0 <= k - 2 < n:
                f_spread(in_a, k - 2)
            if 0 <= k - 3 < n:
                final(k - 3)
                final_send(in_a, k - 3)
            if 0 <= k - 4 < n:
                finish(k - 4)

    @pl.when(is_b)
    def _():
        xi_r, xi_l = xR // 2, xL // 2

        def x_send(first, x_, d, base, k):
            send(in_b, lambda: rc(Bs[k].at[pl.ds(x_ // 2 * 4 + first, 2)],
                                  Br2s[k].at[d, pl.ds(first, 2)], base + k, base + k, dev(x_=x_)))

        def plain_sends(k):
            x_send(2, xR, 0, b2n_p, k)
            x_send(0, xL, 1, b2n_m, k)

        def sum_sends(k):
            wait_recv(Br1s[k].at[pl.ds(0, 2)], b1_p + k)
            add_blocks(Bs[k], xi_r * 4, 2, lambda i: (Br1s[k].at[i],))
            x_send(0, xR, 0, b2a_p, k)
            wait_recv(Br1s[k].at[pl.ds(2, 2)], b1_m + k)
            add_blocks(Bs[k], xi_l * 4 + 2, 2, lambda i: (Br1s[k].at[2 + i],))
            x_send(2, xL, 1, b2a_m, k)

        def start_chunk(k):
            multiply(k, 0)
            multiply(k, 1)

        start_chunk(0)
        plain_sends(0)
        start_chunk(1)
        for k in range(n + 5):
            if k < n:
                sum_sends(k)
            if k + 1 < n:
                plain_sends(k + 1)
            if k + 2 < n:
                start_chunk(k + 2)
            if 0 <= k - 3 < n:
                f_spread(in_b, k - 3)
            if 0 <= k - 4 < n:
                wait_recv(brrows(k - 4, f), fs + k - 4)
                final(k - 4)
                final_send(in_b, k - 4)
            if 0 <= k - 5 < n:
                finish(k - 5)

    for build in common:
        build().wait_send()

    @pl.when(is_a)
    def _():
        for build in in_a:
            build().wait_send()

    @pl.when(is_b)
    def _():
        for build in in_b:
            build().wait_send()

    rot_store.wait()
    for k in chunks:
        for core in range(2):
            u_store(k, core).wait()
    assert ids.count <= SEMS, ids.count


SEMS = 260


def per_device(replica_grads, basis_left, basis_right, first_moment, second_moment):
    any_space = pl.BlockSpec(memory_space=pl.ANY)
    v = pltpu.VMEM
    scratch = [
        v((ROWS, COLS), BF16),
        v((HALF, COLS), BF16),
        v((HALF, COLS), BF16),
        v((8, ROWS, COLS), BF16),
        v((8, COLS, COLS), BF16),
        v((ROWS, 3584), BF16),
        v((1792, ROWS), BF16),
        v((ROWS, COLS), F32),
        v((ROWS, COLS), BF16),
        v((ROWS, COLS), BF16),
        v((ROWS, COLS), BF16),
        v((8 * HALF, YF), BF16),
        v((8 * HALF, COLS - YF), BF16),
        v((2, HALF, YF), BF16),
        v((2, 2, HALF, YF), BF16),
        v((HALF, YF), BF16),
        v((HALF, COLS), F32),
        v((HALF, YF), BF16),
        v((4, HALF, COLS - YF), BF16),
        v((2, SUB, COLS - YF), BF16),
        v((2, HALF, COLS - YF), BF16),
        v((HALF, COLS), F32),
        v((HALF, COLS), F32),
        v((ROWS, COLS), BF16),
        [v((8, ROWS, w), BF16) for w in WIDTHS],
        [v((4, ROWS, w), BF16) for w in WIDTHS],
        [v((2, 4, ROWS, w), BF16) for w in WIDTHS],
        [v((3, ROWS, w), BF16) for w in WIDTHS],
        [v((ROWS, w), BF16) for w in WIDTHS],
        [v((8 * HALF, w), BF16) for w in WIDTHS],
        [v((2, ROWS, w), F32) for w in WIDTHS],
        pltpu.SemaphoreType.DMA((SEMS,)),
        pltpu.SemaphoreType.DMA((SEMS,)),
        pltpu.SemaphoreType.DMA((6 + 2 * len(WIDTHS),)),
    ]
    rotated, partials = pl.pallas_call(
        kernel,
        out_shape=(
            jax.ShapeDtypeStruct((HALF, COLS), F32),
            jax.ShapeDtypeStruct((2, ROWS, COLS), F32),
        ),
        in_specs=[any_space] * 5,
        out_specs=(any_space,) * 2,
        scratch_shapes=scratch,
        compiler_params=pltpu.CompilerParams(
            collective_id=0, has_side_effects=True, vmem_limit_bytes=60 * 2**20
        ),
        cost_estimate=pl.CostEstimate(
            flops=9 * 10**9, bytes_accessed=10 * 2**20, transcendentals=HALF * COLS
        ),
        name="soap_step",
    )(replica_grads, basis_left, basis_right, first_moment, second_moment)
    first_next = beta_first * first_moment + (1.0 - beta_first) * rotated
    second_next = beta_second * second_moment + (1.0 - beta_second) * rotated * rotated
    return (first_next, second_next, partials[0] + partials[1])


def solution(mesh):
    placed = (
        P("dp", "fsdp", "tensor"),
        P("fsdp", None),
        P("fsdp", "tensor"),
        P(("dp", "fsdp"), "tensor"),
        P(("dp", "fsdp"), "tensor"),
    )
    return jax.shard_map(
        per_device,
        mesh=mesh,
        in_specs=placed,
        out_specs=(P(("dp", "fsdp"), "tensor"), P(("dp", "fsdp"), "tensor"), P("fsdp", "tensor")),
        check_vma=False,
    )
```

```python
import functools

import jax
import jax.numpy as jnp
from jax import lax
from jax.experimental import pallas as pl
from jax.experimental.pallas import tpu as pltpu
from jax.sharding import PartitionSpec as P

MESH = pl.DeviceIdType.MESH
F32 = jnp.float32
BF16 = jnp.bfloat16

ADAM_STEP = 10
beta_first = 0.9
beta_second = 0.95
epsilon = 1e-08

ROWS = 448
HALF = 224
COLS = 640
SUB = 112
YF = 384
WIDTHS = (128, 128, 128, 128, 128)


class Ids:
    def __init__(self):
        self.table = {}
        self.count = 0

    def get(self, name, width=1):
        if name not in self.table:
            self.table[name] = self.count
            self.count += width
        return self.table[name]


def kernel(
    g_hbm, ql_hbm, qr_hbm, m1_hbm, m2_hbm,
    rot_hbm, u_hbm,
    gv, gx, gs, Gq, G, Q, QL, QT, T, Tse, Tre, Tsl, Trl, Tb, P0, P1, Pr1, Pr2, Rs, Rf, Rr, Zp, Sy1, Sy2,
    m1, m2, D, Bs, Br1s, Br2s, Zrs, brs, brgs, Us,
    ssem, rsem, lsem,
):
    ids = Ids()
    c = lax.axis_index("dp")
    f = lax.axis_index("fsdp")
    t = lax.axis_index("tensor")
    zl, y = f // 4, f % 4
    zh, x = t // 4, t % 4
    p = x % 2
    is_a = c == p
    is_b = c != p
    oc = 1 - c
    yR, yL, yO = (y + 1) % 4, (y + 3) % 4, (y + 2) % 4
    xR, xL, xO = (x + 1) % 4, (x + 3) % 4, (x + 2) % 4
    zR, zL, zO = (zh + 1) % 4, (zh + 3) % 4, (zh + 2) % 4
    zlO = 1 - zl
    fO = zlO * 4 + y

    def dev(core=c, zl_=zl, y_=y, zh_=zh, x_=x):
        return (core, zl_ * 4 + y_, zh_ * 4 + x_)

    def rc(src, dst, sid, rid, device):
        return pltpu.make_async_remote_copy(
            src_ref=src, dst_ref=dst, send_sem=ssem.at[sid], recv_sem=rsem.at[rid],
            device_id=device, device_id_type=MESH,
        )

    common, in_a, in_b = [], [], []

    def send(to, build):
        build().start()
        to.append(build)

    def wait_recv(dst, rid):
        rc(dst, dst, 0, rid, dev(core=oc)).wait_recv()

    def half(h):
        return pl.ds(pl.multiple_of(h * HALF, 16), HALF)

    qr_load = pltpu.make_async_copy(
        qr_hbm.at[pl.ds(pl.multiple_of(c * COLS, COLS), COLS)], Q.at[f], lsem.at[0])
    g_load = pltpu.make_async_copy(g_hbm.at[0], gv, lsem.at[1])
    ql_load = pltpu.make_async_copy(ql_hbm, QL, lsem.at[2])
    m1_load = pltpu.make_async_copy(m1_hbm, m1, lsem.at[3])
    m2_load = pltpu.make_async_copy(m2_hbm, m2, lsem.at[4])
    g_load.start()
    qr_load.start()
    ql_load.start()
    m1_load.start()
    m2_load.start()

    barrier = pltpu.get_barrier_semaphore()
    friends = [dev(core=oc), dev(zh_=zO)]
    for core in (c, oc):
        friends += [dev(core=core, x_=xR), dev(core=core, x_=xL), dev(core=core, y_=yR), dev(core=core, y_=yL), dev(core=core, zl_=zlO),
                    dev(core=core, zh_=zR), dev(core=core, zh_=zL)]
    for friend in friends:
        pl.semaphore_signal(barrier, inc=1, device_id=friend, device_id_type=MESH)
    pl.semaphore_wait(barrier, len(friends))

    g_load.wait()
    send(common, lambda: rc(gv.at[half(oc)], gx, ids.get("g"), ids.get("g"), dev(core=oc)))
    qr_load.wait()

    def qpart(slot, a):
        return Q.at[slot, pl.ds(a * 320, 320)]

    def qsend(name, slot, a, device):
        i = ids.get(name)
        send(common, lambda: rc(qpart(slot, a), qpart(slot, a), i, i, device))

    def qy_own(a):
        qsend(("Qy+", "own", a), f, a, dev(y_=yR))
        qsend(("Qy-", "own", a), f, a, dev(y_=yL))

    def qz_send(a):
        qsend(("Qz", a), f, a, dev(zl_=zlO))

    qy_own(0)
    qz_send(0)
    qy_own(1)

    wait_recv(gx, ids.get("g"))
    gs[...] = (gv[half(c), :].astype(F32) + gx[...].astype(F32)).astype(BF16)

    own = 2 * zh + x // 2

    def gpart(slot, h):
        return G.at[slot, half(h)]

    gz_p, gz_m, gz_o = ids.get("Gz+", 2), ids.get("Gz-", 2), ids.get("Gzo", 2)
    send(common, lambda: rc(gs, gpart(own, c), gz_p + c, gz_p + c, dev(core=p, zh_=zR)))
    send(common, lambda: rc(gs, gpart(own, c), gz_m + c, gz_m + c, dev(core=p, zh_=zL)))
    gx_p, gx_m = ids.get("Gx+", 8), ids.get("Gx-", 8)
    zq = [zh, zL, zR, zO]
    gf_p, gf_m = ids.get("Gxf+", 4), ids.get("Gxf-", 4)
    id_gs, id_gs3 = ids.get("Gs"), ids.get("Gs3")

    def gslot(q, x_):
        return 2 * zq[q] + x_ // 2

    def a_spread(q, h, src=None):
        for base, x_ in ((gx_p, xR), (gx_m, xL)):
            send(in_a, lambda base=base, x_=x_: rc(
                gpart(gslot(q, x), h) if src is None else src, gpart(gslot(q, x), h),
                base + 2 * q + h, base + 2 * q + h, dev(x_=x_)))

    def b_spread(q, src):
        for base, x_ in ((gx_p, xR), (gx_m, xL)):
            send(in_b, lambda base=base, x_=x_: rc(
                src, gpart(gslot(q, x), c), base + 2 * q + c, base + 2 * q + c, dev(core=oc, x_=x_)))

    def qy_own_forward():
        i = ids.get(("Qy+", "own", 0))
        wait_recv(qpart(zl * 4 + yL, 0), i)
        qsend(("Qyf+", "own"), zl * 4 + yL, 0, dev(y_=yR))
        i = ids.get(("Qy-", "own", 1))
        wait_recv(qpart(zl * 4 + yR, 1), i)
        qsend(("Qyf-", "own"), zl * 4 + yR, 1, dev(y_=yL))

    def qz_spread(a):
        wait_recv(qpart(fO, a), ids.get(("Qz", a)))
        qsend(("Qy+", "par", a), fO, a, dev(y_=yR))
        qsend(("Qy-", "par", a), fO, a, dev(y_=yL))

    def transpose_left(group):
        start = pl.multiple_of(c * 1792 + group * 896, 128)
        QT[pl.ds(group * 896, 896), :] = QL[:, pl.ds(start, 896)].T

    def qz_opposite():
        wait_recv(qpart(zl * 4 + yO, 1), ids.get(("Qyf-", "own")))
        i = ids.get("Qzo")
        send(common, lambda: rc(qpart(zl * 4 + yO, 1), qpart(zl * 4 + yO, 1), i, i, dev(zl_=zlO)))

    def quarter(slot, a):
        return Q.at[slot, pl.ds(a * 160, 160)]

    def qy_par_forward():
        wait_recv(qpart(zlO * 4 + yL, 0), ids.get(("Qy+", "par", 0)))
        i = ids.get(("Qyf+", "par"))
        send(common, lambda: rc(quarter(zlO * 4 + yL, 0), quarter(zlO * 4 + yL, 0), i, i, dev(y_=yR)))
        wait_recv(qpart(zlO * 4 + yR, 0), ids.get(("Qy-", "par", 0)))
        j = ids.get(("Qyf-", "par"))
        send(common, lambda: rc(quarter(zlO * 4 + yR, 1), quarter(zlO * 4 + yR, 1), j, j, dev(y_=yL)))

    def b_forward(q, h):
        if h == 0:
            wait_recv(gpart(gslot(q, xL), 0), gx_p + 2 * q)
            send(in_b, lambda: rc(gpart(gslot(q, xL), 0), gpart(gslot(q, xL), 0), gf_p + q, gf_p + q, dev(x_=xR)))
        else:
            wait_recv(gpart(gslot(q, xR), 1), gx_m + 2 * q + 1)
            send(in_b, lambda: rc(gpart(gslot(q, xR), 1), gpart(gslot(q, xR), 1), gf_m + q, gf_m + q, dev(x_=xL)))

    @pl.when(is_a)
    def _():
        send(in_a, lambda: rc(gs, gpart(own, c), gz_o + c, gz_o + c, dev(zh_=zO)))
        a_spread(0, c, src=gs)
        G[own, half(c), :] = gs[...]
        wait_recv(gpart(gslot(1, x), 0), gz_p + 0)
        a_spread(1, 0)
        wait_recv(gpart(gslot(2, x), 1), gz_m + 1)
        a_spread(2, 1)

    @pl.when(is_b)
    def _():
        send(in_b, lambda: rc(gs, Gq, gz_o + c, gz_o + c, dev(zh_=zO)))
        b_spread(0, gs)
        send(in_b, lambda: rc(gs, gpart(own, c), id_gs, id_gs, dev(core=oc)))
        b_forward(0, 0)
        b_forward(0, 1)

    qz_send(1)
    ql_load.wait()
    transpose_left(0)

    @pl.when(is_a)
    def _():
        wait_recv(gpart(gslot(1, x), 1), gz_p + 1)
        a_spread(1, 1)
        wait_recv(gpart(gslot(2, x), 0), gz_m + 0)
        a_spread(2, 0)

    qy_own_forward()

    @pl.when(is_a)
    def _():
        wait_recv(gpart(gslot(3, x), c), gz_o + c)
        a_spread(3, c)

    @pl.when(is_b)
    def _():
        b_forward(1, 0)
        wait_recv(Gq, gz_o + c)
        b_spread(3, Gq)
        send(in_b, lambda: rc(Gq, gpart(gslot(3, x), c), id_gs3, id_gs3, dev(core=oc)))
        b_forward(2, 1)

    qz_spread(0)

    @pl.when(is_b)
    def _():
        b_forward(1, 1)
        b_forward(2, 0)

    qz_spread(1)
    transpose_left(1)

    @pl.when(is_b)
    def _():
        b_forward(3, 0)
        b_forward(3, 1)

    qz_opposite()
    qy_par_forward()

    @pl.when(is_b)
    def _():
        for q in range(4):
            wait_recv(gpart(gslot(q, xL), 1), gx_p + 2 * q + 1)
            wait_recv(gpart(gslot(q, xR), 0), gx_m + 2 * q)

    @pl.when(is_a)
    def _():
        wait_recv(gpart(own, oc), id_gs)
        wait_recv(gpart(gslot(3, x), oc), id_gs3)
        for q in range(4):
            wait_recv(gpart(gslot(q, xO), 0), gf_p + q)
            wait_recv(gpart(gslot(q, xO), 1), gf_m + q)

    def psend(name, src, dst, device):
        i = ids.get(name)
        send(common, lambda: rc(src, dst, i, i, device))

    T[...] = jnp.zeros_like(T)
    last = zlO * 4 + yO

    def accumulate(slot):
        T[...] += jnp.dot(G[slot], Q[slot], preferred_element_type=F32)

    wait_recv(qpart(zl * 4 + yL, 1), ids.get(("Qy+", "own", 1)))
    wait_recv(qpart(zl * 4 + yR, 0), ids.get(("Qy-", "own", 0)))
    wait_recv(qpart(zl * 4 + yO, 0), ids.get(("Qyf+", "own")))

    @pl.loop(0, 4)
    def _(i):
        accumulate(zl * 4 + i)

    accumulate(fO)
    wait_recv(qpart(zlO * 4 + yL, 1), ids.get(("Qy+", "par", 1)))
    wait_recv(qpart(zlO * 4 + yR, 1), ids.get(("Qy-", "par", 1)))

    @pl.loop(0, 2)
    def _(i):
        accumulate(zlO * 4 + (y + 1 + 2 * i) % 4)

    wait_recv(quarter(last, 0), ids.get(("Qyf+", "par")))
    wait_recv(quarter(last, 1), ids.get(("Qyf-", "par")))
    wait_recv(qpart(last, 1), ids.get("Qzo"))
    early, late = slice(YF, COLS), slice(0, YF)
    for cols, buf, got, name in ((early, Tse, Tre, "Te"), (late, Tsl, Trl, "Tl")):
        T[:, cols] += jnp.dot(G[last], Q[last, :, cols], preferred_element_type=F32)
        buf[...] = T[:, cols].astype(BF16)
        psend(name, buf, got, dev(core=oc))

    def exchanged(got, cols, name):
        wait_recv(got, ids.get(name))
        Tb[:, cols] = (T[:, cols] + got[...].astype(F32)).astype(BF16)

    def left(buf, group, lo, width):
        r = pl.ds(pl.multiple_of(group * 896, 128), 896)
        buf[r, :] = jnp.dot(
            QT[r, :], Tb[:, lo:lo + width], preferred_element_type=F32).astype(BF16)

    def pblock(buf, zl_, y_):
        return buf.at[pl.ds(pl.multiple_of((zl_ * 4 + y_) * HALF, 16), HALF)]

    def spart(y_, s):
        return P1.at[pl.ds(pl.multiple_of((zl * 4 + y_) * HALF + s * SUB, 16), SUB)]

    def half_of(buf, s):
        return buf.at[pl.ds(s * SUB, SUB)]

    def add_into(dst, *others):
        total = dst[...].astype(F32)
        for other in others:
            total = total + other[...].astype(F32)
        dst[...] = total.astype(dst.dtype)

    exchanged(Tre, early, "Te")
    left(P1, zlO, YF, COLS - YF)
    for name, y_ in (("O", yO), ("R", yR), ("L", yL), ("S", y)):
        psend(("Pz1", name), pblock(P1, zlO, y_), Zp.at[y_], dev(zl_=zlO))
    exchanged(Trl, late, "Tl")
    left(P0, 0, 0, YF)
    psend("Py1+", pblock(P0, 0, yO), Pr1.at[0], dev(y_=yR))
    psend("Py2-n", pblock(P0, 0, yL), Pr2.at[1, 0], dev(y_=yL))
    left(P0, 1, 0, YF)
    psend("Py1-", pblock(P0, 1, yO), Pr1.at[1], dev(y_=yL))
    psend("Py2+n", pblock(P0, 1, yR), Pr2.at[0, 1], dev(y_=yR))
    left(P1, zl, YF, COLS - YF)

    def z_add(name, y_):
        wait_recv(Zp.at[y_], ids.get(("Pz1", name)))
        add_into(pblock(P1, zl, y_), Zp.at[y_])

    z_add("O", yO)
    psend("Sy1+", spart(yO, 0), Sy1.at[0], dev(y_=yR))
    psend("Sy1-", spart(yO, 1), Sy1.at[1], dev(y_=yL))
    wait_recv(Pr1.at[0], ids.get("Py1+"))
    add_into(pblock(P0, 0, yR), Pr1.at[0])
    psend("Py2+a", pblock(P0, 0, yR), Pr2.at[0, 0], dev(y_=yR))
    wait_recv(Pr1.at[1], ids.get("Py1-"))
    add_into(pblock(P0, 1, yL), Pr1.at[1])
    psend("Py2-a", pblock(P0, 1, yL), Pr2.at[1, 1], dev(y_=yL))
    z_add("R", yR)
    psend("Sy2+n", spart(yR, 1), half_of(Sy2.at[0], 1), dev(y_=yR))
    wait_recv(Sy1.at[0], ids.get("Sy1+"))
    add_into(spart(yR, 0), Sy1.at[0])
    psend("Sy2+a", spart(yR, 0), half_of(Sy2.at[0], 0), dev(y_=yR))
    z_add("L", yL)
    psend("Sy2-n", spart(yL, 0), half_of(Sy2.at[1], 0), dev(y_=yL))
    wait_recv(Sy1.at[1], ids.get("Sy1-"))
    add_into(spart(yL, 1), Sy1.at[1])
    psend("Sy2-a", spart(yL, 1), half_of(Sy2.at[1], 1), dev(y_=yL))
    wait_recv(Pr2.at[0, 1], ids.get("Py2+n"))
    wait_recv(Pr2.at[1, 0], ids.get("Py2-n"))
    wait_recv(Pr2.at[0, 0], ids.get("Py2+a"))
    wait_recv(Pr2.at[1, 1], ids.get("Py2-a"))

    def block_total(zl_):
        return (pblock(P0, zl_, y)[...].astype(F32) + Pr2[0, zl_].astype(F32)
                + Pr2[1, zl_].astype(F32))

    Rs[...] = block_total(zlO).astype(BF16)
    psend("Pz", Rs, Rr, dev(zl_=zlO))
    Rf[:, 0:YF] = block_total(zl)
    wait_recv(Zp.at[y], ids.get(("Pz1", "S")))
    total = pblock(P1, zl, y)[...].astype(F32) + Zp[y].astype(F32)
    wait_recv(half_of(Sy2.at[0], 0), ids.get("Sy2+a"))
    wait_recv(half_of(Sy2.at[0], 1), ids.get("Sy2+n"))
    wait_recv(half_of(Sy2.at[1], 0), ids.get("Sy2-n"))
    wait_recv(half_of(Sy2.at[1], 1), ids.get("Sy2-a"))
    Rf[:, YF:COLS] = total + Sy2[0].astype(F32) + Sy2[1].astype(F32)
    m1_load.wait()
    m2_load.wait()
    wait_recv(Rr, ids.get("Pz"))

    def adam(r, lo, hi, rotated):
        Rf[r, lo:hi] = rotated
        first = beta_first * m1[r, lo:hi] + (1.0 - beta_first) * rotated
        second = beta_second * m2[r, lo:hi] + (1.0 - beta_second) * rotated * rotated
        first_hat = first / (1.0 - beta_first**ADAM_STEP)
        second_hat = second / (1.0 - beta_second**ADAM_STEP)
        where = pl.ds(pl.multiple_of(c * HALF + r.start, 16), 32)
        D[where, lo:hi] = (first_hat / (jnp.sqrt(second_hat) + epsilon)).astype(BF16)

    @pl.loop(0, HALF // 32)
    def _(i):
        r = pl.ds(pl.multiple_of(i * 32, 32), 32)
        adam(r, 0, YF, Rf[r, 0:YF] + Rr[r, :].astype(F32))
        adam(r, YF, COLS, Rf[r, YF:COLS])

    id_d = ids.get("D")
    send(common, lambda: rc(D.at[half(c)], D.at[half(c)], id_d, id_d, dev(core=oc)))
    rot_store = pltpu.make_async_copy(Rf, rot_hbm, lsem.at[5])
    rot_store.start()
    wait_recv(D.at[half(oc)], id_d)

    chunks = range(len(WIDTHS))
    lows = [sum(WIDTHS[:k]) for k in chunks]
    n = len(WIDTHS)

    def multiply(k, xi):
        @pl.loop(0, 4)
        def _(z):
            Bs[k][xi * 4 + z] = lax.dot_general(
                D[...], Q[2 * z + xi, pl.ds(lows[k], WIDTHS[k])],
                (((1,), (1,)), ((), ())), preferred_element_type=F32
            ).astype(BF16)

    b1_p, b1_m = ids.get("Bx1+", n), ids.get("Bx1-", n)
    b2n_p, b2n_m = ids.get("Bx2+n", n), ids.get("Bx2-n", n)
    b2a_p, b2a_m = ids.get("Bx2+a", n), ids.get("Bx2-a", n)
    z_p, z_m, z_o = ids.get("Bz+", n), ids.get("Bz-", n), ids.get("Bzo", n)
    fs, fz = ids.get("Fs", n), ids.get("Fz", 2 * n)
    fy = [ids.get(("Fy", d), 2 * n) for d in range(3)]
    fp = [ids.get(("Fp", d), n) for d in range(3)]
    id_u = ids.get("U", n)

    ys = (yR, yL, yO)
    sources = (yL, yR, yO)

    def brrows(k, f_):
        return brgs[k].at[pl.ds(pl.multiple_of(f_ * HALF, 16), HALF)]

    def f_spread(to, k):
        wait_recv(brrows(k, fO), fz + k)
        for d in range(3):
            send(to, lambda d=d: rc(brrows(k, fO), brrows(k, fO), fp[d] + k, fp[d] + k, dev(y_=ys[d])))

    def final(k):
        for d in range(3):
            wait_recv(brrows(k, zl * 4 + sources[d]), fy[d] + k)
            wait_recv(brrows(k, zlO * 4 + sources[d]), fp[d] + k)
        start = pl.multiple_of(c * 1792, 128)
        Us[k][c] = jnp.dot(QL[:, pl.ds(start, 1792)], brgs[k][...], preferred_element_type=F32)

    def final_send(to, k):
        send(to, lambda: rc(Us[k].at[c], Us[k].at[c], id_u + k, id_u + k, dev(core=oc)))

    def u_store(k, core):
        return pltpu.make_async_copy(
            Us[k].at[core], u_hbm.at[core, :, pl.ds(lows[k], WIDTHS[k])], lsem.at[6 + 2 * k + core])

    def finish(k):
        u_store(k, c).start()
        wait_recv(Us[k].at[oc], id_u + k)
        u_store(k, oc).start()

    def add_blocks(buf, first, count, terms):
        @pl.loop(0, count)
        def _(i):
            dst = buf.at[first + i]
            total = dst[...].astype(F32)
            for term in terms(i):
                total = total + term[...].astype(F32)
            dst[...] = total.astype(BF16)

    @pl.when(is_a)
    def _():
        xi_own, xi_opp = x // 2, 1 - x // 2

        def opp_sends(k):
            send(in_a, lambda: rc(Bs[k].at[pl.ds((1 - x // 2) * 4, 2)], Br1s[k].at[pl.ds(0, 2)],
                                  b1_p + k, b1_p + k, dev(x_=xR)))
            send(in_a, lambda: rc(Bs[k].at[pl.ds((1 - x // 2) * 4 + 2, 2)], Br1s[k].at[pl.ds(2, 2)],
                                  b1_m + k, b1_m + k, dev(x_=xL)))

        def block(k, z_):
            return Bs[k].at[(x // 2) * 4 + z_]

        def x_total(k):
            wait_recv(Br2s[k].at[0, pl.ds(2, 2)], b2n_p + k)
            wait_recv(Br2s[k].at[1, pl.ds(0, 2)], b2n_m + k)
            wait_recv(Br2s[k].at[0, pl.ds(0, 2)], b2a_p + k)
            wait_recv(Br2s[k].at[1, pl.ds(2, 2)], b2a_m + k)
            add_blocks(Bs[k], xi_own * 4, 4, lambda i: (Br2s[k].at[0, i], Br2s[k].at[1, i]))
            send(in_a, lambda: rc(block(k, zR), Zrs[k].at[0], z_p + k, z_p + k, dev(zh_=zR)))
            send(in_a, lambda: rc(block(k, zL), Zrs[k].at[1], z_m + k, z_m + k, dev(zh_=zL)))
            send(in_a, lambda: rc(block(k, zO), Zrs[k].at[2], z_o + k, z_o + k, dev(zh_=zO)))

        def z_total(k):
            wait_recv(Zrs[k].at[0], z_p + k)
            wait_recv(Zrs[k].at[1], z_m + k)
            wait_recv(Zrs[k].at[2], z_o + k)
            brs[k][...] = (Bs[k][(x // 2) * 4 + zh].astype(F32) + Zrs[k][0].astype(F32)
                           + Zrs[k][1].astype(F32) + Zrs[k][2].astype(F32)).astype(BF16)
            for other in range(2):
                def src(other=other):
                    return brs[k].at[half(oc if other else c)]

                def to(other=other, **moved):
                    return dev(core=oc if other else c, **moved)

                send(in_a, lambda src=src, to=to, other=other: rc(
                    src(), brrows(k, f), fz + k + n * other, fz + k, to(zl_=zlO)))
                for d in range(3):
                    send(in_a, lambda src=src, to=to, other=other, d=d: rc(
                        src(), brrows(k, f), fy[d] + k + n * other, fy[d] + k, to(y_=ys[d])))
            send(in_a, lambda: rc(brs[k].at[half(oc)], brrows(k, f), fs + k, fs + k, dev(core=oc)))
            brrows(k, f)[...] = brs[k][half(c), :]

        def start_chunk(k):
            multiply(k, xi_opp)
            opp_sends(k)
            multiply(k, xi_own)

        start_chunk(0)
        start_chunk(1)
        for k in range(n + 4):
            if k < n:
                x_total(k)
            if k + 2 < n:
                start_chunk(k + 2)
            if 0 <= k - 1 < n:
                z_total(k - 1)
            if 0 <= k - 2 < n:
                f_spread(in_a, k - 2)
            if 0 <= k - 3 < n:
                final(k - 3)
                final_send(in_a, k - 3)
            if 0 <= k - 4 < n:
                finish(k - 4)

    @pl.when(is_b)
    def _():
        xi_r, xi_l = xR // 2, xL // 2

        def x_send(first, x_, d, base, k):
            send(in_b, lambda: rc(Bs[k].at[pl.ds(x_ // 2 * 4 + first, 2)],
                                  Br2s[k].at[d, pl.ds(first, 2)], base + k, base + k, dev(x_=x_)))

        def plain_sends(k):
            x_send(2, xR, 0, b2n_p, k)
            x_send(0, xL, 1, b2n_m, k)

        def sum_sends(k):
            wait_recv(Br1s[k].at[pl.ds(0, 2)], b1_p + k)
            add_blocks(Bs[k], xi_r * 4, 2, lambda i: (Br1s[k].at[i],))
            x_send(0, xR, 0, b2a_p, k)
            wait_recv(Br1s[k].at[pl.ds(2, 2)], b1_m + k)
            add_blocks(Bs[k], xi_l * 4 + 2, 2, lambda i: (Br1s[k].at[2 + i],))
            x_send(2, xL, 1, b2a_m, k)

        def start_chunk(k):
            multiply(k, 0)
            multiply(k, 1)

        start_chunk(0)
        plain_sends(0)
        start_chunk(1)
        for k in range(n + 5):
            if k < n:
                sum_sends(k)
            if k + 1 < n:
                plain_sends(k + 1)
            if k + 2 < n:
                start_chunk(k + 2)
            if 0 <= k - 3 < n:
                f_spread(in_b, k - 3)
            if 0 <= k - 4 < n:
                wait_recv(brrows(k - 4, f), fs + k - 4)
                final(k - 4)
                final_send(in_b, k - 4)
            if 0 <= k - 5 < n:
                finish(k - 5)

    for build in common:
        build().wait_send()

    @pl.when(is_a)
    def _():
        for build in in_a:
            build().wait_send()

    @pl.when(is_b)
    def _():
        for build in in_b:
            build().wait_send()

    rot_store.wait()
    for k in chunks:
        for core in range(2):
            u_store(k, core).wait()
    assert ids.count <= SEMS, ids.count


SEMS = 260


def per_device(replica_grads, basis_left, basis_right, first_moment, second_moment):
    any_space = pl.BlockSpec(memory_space=pl.ANY)
    v = pltpu.VMEM
    scratch = [
        v((ROWS, COLS), BF16),
        v((HALF, COLS), BF16),
        v((HALF, COLS), BF16),
        v((HALF, COLS), BF16),
        v((8, ROWS, COLS), BF16),
        v((8, COLS, COLS), BF16),
        v((ROWS, 3584), BF16),
        v((1792, ROWS), BF16),
        v((ROWS, COLS), F32),
        v((ROWS, COLS - YF), BF16),
        v((ROWS, COLS - YF), BF16),
        v((ROWS, YF), BF16),
        v((ROWS, YF), BF16),
        v((ROWS, COLS), BF16),
        v((8 * HALF, YF), BF16),
        v((8 * HALF, COLS - YF), BF16),
        v((2, HALF, YF), BF16),
        v((2, 2, HALF, YF), BF16),
        v((HALF, YF), BF16),
        v((HALF, COLS), F32),
        v((HALF, YF), BF16),
        v((4, HALF, COLS - YF), BF16),
        v((2, SUB, COLS - YF), BF16),
        v((2, HALF, COLS - YF), BF16),
        v((HALF, COLS), F32),
        v((HALF, COLS), F32),
        v((ROWS, COLS), BF16),
        [v((8, ROWS, w), BF16) for w in WIDTHS],
        [v((4, ROWS, w), BF16) for w in WIDTHS],
        [v((2, 4, ROWS, w), BF16) for w in WIDTHS],
        [v((3, ROWS, w), BF16) for w in WIDTHS],
        [v((ROWS, w), BF16) for w in WIDTHS],
        [v((8 * HALF, w), BF16) for w in WIDTHS],
        [v((2, ROWS, w), F32) for w in WIDTHS],
        pltpu.SemaphoreType.DMA((SEMS,)),
        pltpu.SemaphoreType.DMA((SEMS,)),
        pltpu.SemaphoreType.DMA((6 + 2 * len(WIDTHS),)),
    ]
    rotated, partials = pl.pallas_call(
        kernel,
        out_shape=(
            jax.ShapeDtypeStruct((HALF, COLS), F32),
            jax.ShapeDtypeStruct((2, ROWS, COLS), F32),
        ),
        in_specs=[any_space] * 5,
        out_specs=(any_space,) * 2,
        scratch_shapes=scratch,
        compiler_params=pltpu.CompilerParams(
            collective_id=0, has_side_effects=True, vmem_limit_bytes=60 * 2**20
        ),
        cost_estimate=pl.CostEstimate(
            flops=9 * 10**9, bytes_accessed=10 * 2**20, transcendentals=HALF * COLS
        ),
        name="soap_step",
    )(replica_grads, basis_left, basis_right, first_moment, second_moment)
    first_next = beta_first * first_moment + (1.0 - beta_first) * rotated
    second_next = beta_second * second_moment + (1.0 - beta_second) * rotated * rotated
    return (first_next, second_next, partials[0] + partials[1])


def solution(mesh):
    placed = (
        P("dp", "fsdp", "tensor"),
        P("fsdp", None),
        P("fsdp", "tensor"),
        P(("dp", "fsdp"), "tensor"),
        P(("dp", "fsdp"), "tensor"),
    )
    return jax.shard_map(
        per_device,
        mesh=mesh,
        in_specs=placed,
        out_specs=(P(("dp", "fsdp"), "tensor"), P(("dp", "fsdp"), "tensor"), P("fsdp", "tensor")),
        check_vma=False,
    )
```

```python
import functools

import jax
import jax.numpy as jnp
from jax import lax
from jax.experimental import pallas as pl
from jax.experimental.pallas import tpu as pltpu
from jax.sharding import PartitionSpec as P

MESH = pl.DeviceIdType.MESH
F32 = jnp.float32
BF16 = jnp.bfloat16

ADAM_STEP = 10
beta_first = 0.9
beta_second = 0.95
epsilon = 1e-08

ROWS = 448
HALF = 224
COLS = 640
SUB = 112
YF = 384
WIDTHS = (128, 128, 128, 128, 128)


class Ids:
    def __init__(self):
        self.table = {}
        self.count = 0

    def get(self, name, width=1):
        if name not in self.table:
            self.table[name] = self.count
            self.count += width
        return self.table[name]


def kernel(
    g_hbm, ql_hbm, qr_hbm, m1_hbm, m2_hbm,
    rot_hbm, u_hbm,
    gv, gx, gs, Gq, G, Q, QL, QT, T, Tse, Tre, Tsl, Trl, Tb, P0, P1, Pr1, Pr2, Rs, Rf, Rr, Zp, Sy1, Sy2,
    m1, m2, D, Bs, Br1s, Br2s, Zrs, brs, brgs, Us,
    ssem, rsem, lsem,
):
    ids = Ids()
    c = lax.axis_index("dp")
    f = lax.axis_index("fsdp")
    t = lax.axis_index("tensor")
    zl, y = f // 4, f % 4
    zh, x = t // 4, t % 4
    p = x % 2
    is_a = c == p
    is_b = c != p
    oc = 1 - c
    yR, yL, yO = (y + 1) % 4, (y + 3) % 4, (y + 2) % 4
    xR, xL, xO = (x + 1) % 4, (x + 3) % 4, (x + 2) % 4
    zR, zL, zO = (zh + 1) % 4, (zh + 3) % 4, (zh + 2) % 4
    zlO = 1 - zl
    fO = zlO * 4 + y

    def dev(core=c, zl_=zl, y_=y, zh_=zh, x_=x):
        return (core, zl_ * 4 + y_, zh_ * 4 + x_)

    def rc(src, dst, sid, rid, device):
        return pltpu.make_async_remote_copy(
            src_ref=src, dst_ref=dst, send_sem=ssem.at[sid], recv_sem=rsem.at[rid],
            device_id=device, device_id_type=MESH,
        )

    common, in_a, in_b = [], [], []

    def send(to, build):
        build().start()
        to.append(build)

    def wait_recv(dst, rid):
        rc(dst, dst, 0, rid, dev(core=oc)).wait_recv()

    def half(h):
        return pl.ds(pl.multiple_of(h * HALF, 16), HALF)

    qr_load = pltpu.make_async_copy(
        qr_hbm.at[pl.ds(pl.multiple_of(c * COLS, COLS), COLS)], Q.at[f], lsem.at[0])
    g_load = pltpu.make_async_copy(g_hbm.at[0], gv, lsem.at[1])
    ql_load = pltpu.make_async_copy(ql_hbm, QL, lsem.at[2])
    m1_load = pltpu.make_async_copy(m1_hbm, m1, lsem.at[3])
    m2_load = pltpu.make_async_copy(m2_hbm, m2, lsem.at[4])
    g_load.start()
    qr_load.start()
    ql_load.start()
    m1_load.start()
    m2_load.start()

    barrier = pltpu.get_barrier_semaphore()
    friends = [dev(core=oc), dev(zh_=zO)]
    for core in (c, oc):
        friends += [dev(core=core, x_=xR), dev(core=core, x_=xL), dev(core=core, y_=yR), dev(core=core, y_=yL), dev(core=core, zl_=zlO),
                    dev(core=core, zh_=zR), dev(core=core, zh_=zL)]
    for friend in friends:
        pl.semaphore_signal(barrier, inc=1, device_id=friend, device_id_type=MESH)
    pl.semaphore_wait(barrier, len(friends))

    g_load.wait()
    send(common, lambda: rc(gv.at[half(oc)], gx, ids.get("g"), ids.get("g"), dev(core=oc)))
    qr_load.wait()

    def qpart(slot, a):
        return Q.at[slot, pl.ds(a * 320, 320)]

    def qsend(name, slot, a, device):
        i = ids.get(name)
        send(common, lambda: rc(qpart(slot, a), qpart(slot, a), i, i, device))

    def qy_own(a):
        qsend(("Qy+", "own", a), f, a, dev(y_=yR))
        qsend(("Qy-", "own", a), f, a, dev(y_=yL))

    def qz_send(a):
        qsend(("Qz", a), f, a, dev(zl_=zlO))

    qy_own(0)
    qz_send(0)
    qy_own(1)

    wait_recv(gx, ids.get("g"))
    gs[...] = (gv[half(c), :].astype(F32) + gx[...].astype(F32)).astype(BF16)

    own = 2 * zh + x // 2

    def gpart(slot, h):
        return G.at[slot, half(h)]

    gz_p, gz_m, gz_o = ids.get("Gz+", 2), ids.get("Gz-", 2), ids.get("Gzo", 2)
    send(common, lambda: rc(gs, gpart(own, c), gz_p + c, gz_p + c, dev(core=p, zh_=zR)))
    send(common, lambda: rc(gs, gpart(own, c), gz_m + c, gz_m + c, dev(core=p, zh_=zL)))
    gx_p, gx_m = ids.get("Gx+", 8), ids.get("Gx-", 8)
    zq = [zh, zL, zR, zO]
    gf_p, gf_m = ids.get("Gxf+", 4), ids.get("Gxf-", 4)
    id_gs, id_gs3 = ids.get("Gs"), ids.get("Gs3")

    def gslot(q, x_):
        return 2 * zq[q] + x_ // 2

    def a_spread(q, h, src=None):
        for base, x_ in ((gx_p, xR), (gx_m, xL)):
            send(in_a, lambda base=base, x_=x_: rc(
                gpart(gslot(q, x), h) if src is None else src, gpart(gslot(q, x), h),
                base + 2 * q + h, base + 2 * q + h, dev(x_=x_)))

    def b_spread(q, src):
        for base, x_ in ((gx_p, xR), (gx_m, xL)):
            send(in_b, lambda base=base, x_=x_: rc(
                src, gpart(gslot(q, x), c), base + 2 * q + c, base + 2 * q + c, dev(core=oc, x_=x_)))

    def qy_own_forward():
        i = ids.get(("Qy+", "own", 0))
        wait_recv(qpart(zl * 4 + yL, 0), i)
        qsend(("Qyf+", "own"), zl * 4 + yL, 0, dev(y_=yR))
        i = ids.get(("Qy-", "own", 1))
        wait_recv(qpart(zl * 4 + yR, 1), i)
        qsend(("Qyf-", "own"), zl * 4 + yR, 1, dev(y_=yL))

    def qz_spread(a):
        wait_recv(qpart(fO, a), ids.get(("Qz", a)))
        qsend(("Qy+", "par", a), fO, a, dev(y_=yR))
        qsend(("Qy-", "par", a), fO, a, dev(y_=yL))

    def transpose_left(group):
        start = pl.multiple_of(c * 1792 + group * 896, 128)
        QT[pl.ds(group * 896, 896), :] = QL[:, pl.ds(start, 896)].T

    def qz_opposite():
        wait_recv(qpart(zl * 4 + yO, 1), ids.get(("Qyf-", "own")))
        i = ids.get("Qzo")
        send(common, lambda: rc(qpart(zl * 4 + yO, 1), qpart(zl * 4 + yO, 1), i, i, dev(zl_=zlO)))

    def quarter(slot, a):
        return Q.at[slot, pl.ds(a * 160, 160)]

    def qy_par_forward():
        wait_recv(qpart(zlO * 4 + yL, 0), ids.get(("Qy+", "par", 0)))
        i = ids.get(("Qyf+", "par"))
        send(common, lambda: rc(quarter(zlO * 4 + yL, 0), quarter(zlO * 4 + yL, 0), i, i, dev(y_=yR)))
        wait_recv(qpart(zlO * 4 + yR, 0), ids.get(("Qy-", "par", 0)))
        j = ids.get(("Qyf-", "par"))
        send(common, lambda: rc(quarter(zlO * 4 + yR, 1), quarter(zlO * 4 + yR, 1), j, j, dev(y_=yL)))

    def b_forward(q, h):
        if h == 0:
            wait_recv(gpart(gslot(q, xL), 0), gx_p + 2 * q)
            send(in_b, lambda: rc(gpart(gslot(q, xL), 0), gpart(gslot(q, xL), 0), gf_p + q, gf_p + q, dev(x_=xR)))
        else:
            wait_recv(gpart(gslot(q, xR), 1), gx_m + 2 * q + 1)
            send(in_b, lambda: rc(gpart(gslot(q, xR), 1), gpart(gslot(q, xR), 1), gf_m + q, gf_m + q, dev(x_=xL)))

    @pl.when(is_a)
    def _():
        send(in_a, lambda: rc(gs, gpart(own, c), gz_o + c, gz_o + c, dev(zh_=zO)))
        a_spread(0, c, src=gs)
        G[own, half(c), :] = gs[...]
        wait_recv(gpart(gslot(1, x), 0), gz_p + 0)
        a_spread(1, 0)
        wait_recv(gpart(gslot(2, x), 1), gz_m + 1)
        a_spread(2, 1)

    @pl.when(is_b)
    def _():
        send(in_b, lambda: rc(gs, Gq, gz_o + c, gz_o + c, dev(zh_=zO)))
        b_spread(0, gs)
        send(in_b, lambda: rc(gs, gpart(own, c), id_gs, id_gs, dev(core=oc)))
        b_forward(0, 0)
        b_forward(0, 1)

    qz_send(1)
    ql_load.wait()
    transpose_left(0)

    @pl.when(is_a)
    def _():
        wait_recv(gpart(gslot(1, x), 1), gz_p + 1)
        a_spread(1, 1)
        wait_recv(gpart(gslot(2, x), 0), gz_m + 0)
        a_spread(2, 0)

    qy_own_forward()

    @pl.when(is_a)
    def _():
        wait_recv(gpart(gslot(3, x), c), gz_o + c)
        a_spread(3, c)

    @pl.when(is_b)
    def _():
        b_forward(1, 0)
        wait_recv(Gq, gz_o + c)
        b_spread(3, Gq)
        send(in_b, lambda: rc(Gq, gpart(gslot(3, x), c), id_gs3, id_gs3, dev(core=oc)))
        b_forward(2, 1)

    qz_spread(0)

    @pl.when(is_b)
    def _():
        b_forward(1, 1)
        b_forward(2, 0)

    qz_spread(1)
    transpose_left(1)

    @pl.when(is_b)
    def _():
        b_forward(3, 0)
        b_forward(3, 1)

    qz_opposite()
    qy_par_forward()

    @pl.when(is_b)
    def _():
        for q in range(4):
            wait_recv(gpart(gslot(q, xL), 1), gx_p + 2 * q + 1)
            wait_recv(gpart(gslot(q, xR), 0), gx_m + 2 * q)

    @pl.when(is_a)
    def _():
        wait_recv(gpart(own, oc), id_gs)
        wait_recv(gpart(gslot(3, x), oc), id_gs3)
        for q in range(4):
            wait_recv(gpart(gslot(q, xO), 0), gf_p + q)
            wait_recv(gpart(gslot(q, xO), 1), gf_m + q)

    def psend(name, src, dst, device):
        i = ids.get(name)
        send(common, lambda: rc(src, dst, i, i, device))

    T[...] = jnp.zeros_like(T)
    last = zlO * 4 + yO

    def accumulate(slot):
        T[...] += jnp.dot(G[slot], Q[slot], preferred_element_type=F32)

    wait_recv(qpart(zl * 4 + yL, 1), ids.get(("Qy+", "own", 1)))
    wait_recv(qpart(zl * 4 + yR, 0), ids.get(("Qy-", "own", 0)))
    wait_recv(qpart(zl * 4 + yO, 0), ids.get(("Qyf+", "own")))

    @pl.loop(0, 4)
    def _(i):
        accumulate(zl * 4 + i)

    accumulate(fO)
    wait_recv(qpart(zlO * 4 + yL, 1), ids.get(("Qy+", "par", 1)))
    wait_recv(qpart(zlO * 4 + yR, 1), ids.get(("Qy-", "par", 1)))

    @pl.loop(0, 2)
    def _(i):
        accumulate(zlO * 4 + (y + 1 + 2 * i) % 4)

    wait_recv(quarter(last, 0), ids.get(("Qyf+", "par")))
    wait_recv(quarter(last, 1), ids.get(("Qyf-", "par")))
    wait_recv(qpart(last, 1), ids.get("Qzo"))
    early, late = slice(YF, COLS), slice(0, YF)
    for cols, buf, got, name in ((early, Tse, Tre, "Te"), (late, Tsl, Trl, "Tl")):
        T[:, cols] += jnp.dot(G[last], Q[last, :, cols], preferred_element_type=F32)
        buf[...] = T[:, cols].astype(BF16)
        psend(name, buf, got, dev(core=oc))

    def exchanged(got, cols, name):
        wait_recv(got, ids.get(name))
        Tb[:, cols] = (T[:, cols] + got[...].astype(F32)).astype(BF16)

    def left(buf, group, lo, width):
        r = pl.ds(pl.multiple_of(group * 896, 128), 896)
        buf[r, :] = jnp.dot(
            QT[r, :], Tb[:, lo:lo + width], preferred_element_type=F32).astype(BF16)

    def pblock(buf, zl_, y_):
        return buf.at[pl.ds(pl.multiple_of((zl_ * 4 + y_) * HALF, 16), HALF)]

    def spart(y_, s):
        return P1.at[pl.ds(pl.multiple_of((zl * 4 + y_) * HALF + s * SUB, 16), SUB)]

    def half_of(buf, s):
        return buf.at[pl.ds(s * SUB, SUB)]

    def add_into(dst, *others):
        total = dst[...].astype(F32)
        for other in others:
            total = total + other[...].astype(F32)
        dst[...] = total.astype(dst.dtype)

    exchanged(Tre, early, "Te")
    left(P1, zlO, YF, COLS - YF)
    for name, y_ in (("O", yO), ("R", yR), ("L", yL), ("S", y)):
        psend(("Pz1", name), pblock(P1, zlO, y_), Zp.at[y_], dev(zl_=zlO))
    exchanged(Trl, late, "Tl")
    left(P0, 0, 0, YF)
    psend("Py1+", pblock(P0, 0, yO), Pr1.at[0], dev(y_=yR))
    psend("Py2-n", pblock(P0, 0, yL), Pr2.at[1, 0], dev(y_=yL))
    left(P0, 1, 0, YF)
    psend("Py1-", pblock(P0, 1, yO), Pr1.at[1], dev(y_=yL))
    psend("Py2+n", pblock(P0, 1, yR), Pr2.at[0, 1], dev(y_=yR))
    left(P1, zl, YF, COLS - YF)

    def z_add(name, y_):
        wait_recv(Zp.at[y_], ids.get(("Pz1", name)))
        add_into(pblock(P1, zl, y_), Zp.at[y_])

    z_add("O", yO)
    psend("Sy1+", spart(yO, 0), Sy1.at[0], dev(y_=yR))
    psend("Sy1-", spart(yO, 1), Sy1.at[1], dev(y_=yL))
    wait_recv(Pr1.at[0], ids.get("Py1+"))
    add_into(pblock(P0, 0, yR), Pr1.at[0])
    psend("Py2+a", pblock(P0, 0, yR), Pr2.at[0, 0], dev(y_=yR))
    wait_recv(Pr1.at[1], ids.get("Py1-"))
    add_into(pblock(P0, 1, yL), Pr1.at[1])
    psend("Py2-a", pblock(P0, 1, yL), Pr2.at[1, 1], dev(y_=yL))
    z_add("R", yR)
    psend("Sy2+n", spart(yR, 1), half_of(Sy2.at[0], 1), dev(y_=yR))
    wait_recv(Sy1.at[0], ids.get("Sy1+"))
    add_into(spart(yR, 0), Sy1.at[0])
    psend("Sy2+a", spart(yR, 0), half_of(Sy2.at[0], 0), dev(y_=yR))
    z_add("L", yL)
    psend("Sy2-n", spart(yL, 0), half_of(Sy2.at[1], 0), dev(y_=yL))
    wait_recv(Sy1.at[1], ids.get("Sy1-"))
    add_into(spart(yL, 1), Sy1.at[1])
    psend("Sy2-a", spart(yL, 1), half_of(Sy2.at[1], 1), dev(y_=yL))
    wait_recv(Pr2.at[0, 1], ids.get("Py2+n"))
    wait_recv(Pr2.at[1, 0], ids.get("Py2-n"))
    wait_recv(Pr2.at[0, 0], ids.get("Py2+a"))
    wait_recv(Pr2.at[1, 1], ids.get("Py2-a"))

    def block_total(zl_):
        return (pblock(P0, zl_, y)[...].astype(F32) + Pr2[0, zl_].astype(F32)
                + Pr2[1, zl_].astype(F32))

    Rs[...] = block_total(zlO).astype(BF16)
    psend("Pz", Rs, Rr, dev(zl_=zlO))
    Rf[:, 0:YF] = block_total(zl)
    wait_recv(Zp.at[y], ids.get(("Pz1", "S")))
    total = pblock(P1, zl, y)[...].astype(F32) + Zp[y].astype(F32)
    wait_recv(half_of(Sy2.at[0], 0), ids.get("Sy2+a"))
    wait_recv(half_of(Sy2.at[0], 1), ids.get("Sy2+n"))
    wait_recv(half_of(Sy2.at[1], 0), ids.get("Sy2-n"))
    wait_recv(half_of(Sy2.at[1], 1), ids.get("Sy2-a"))
    Rf[:, YF:COLS] = total + Sy2[0].astype(F32) + Sy2[1].astype(F32)
    m1_load.wait()
    m2_load.wait()
    wait_recv(Rr, ids.get("Pz"))

    def adam(r, lo, hi, rotated):
        Rf[r, lo:hi] = rotated
        first = beta_first * m1[r, lo:hi] + (1.0 - beta_first) * rotated
        second = beta_second * m2[r, lo:hi] + (1.0 - beta_second) * rotated * rotated
        first_hat = first / (1.0 - beta_first**ADAM_STEP)
        second_hat = second / (1.0 - beta_second**ADAM_STEP)
        where = pl.ds(pl.multiple_of(c * HALF + r.start, 16), 32)
        D[where, lo:hi] = (first_hat / (jnp.sqrt(second_hat) + epsilon)).astype(BF16)

    @pl.loop(0, HALF // 32)
    def _(i):
        r = pl.ds(pl.multiple_of(i * 32, 32), 32)
        adam(r, 0, YF, Rf[r, 0:YF] + Rr[r, :].astype(F32))
        adam(r, YF, COLS, Rf[r, YF:COLS])

    id_d = ids.get("D")
    send(common, lambda: rc(D.at[half(c)], D.at[half(c)], id_d, id_d, dev(core=oc)))
    rot_store = pltpu.make_async_copy(Rf, rot_hbm, lsem.at[5])
    rot_store.start()
    wait_recv(D.at[half(oc)], id_d)

    chunks = range(len(WIDTHS))
    lows = [sum(WIDTHS[:k]) for k in chunks]
    n = len(WIDTHS)

    def multiply(k, xi):
        @pl.loop(0, 4)
        def _(z):
            Bs[k][xi * 4 + z] = lax.dot_general(
                D[...], Q[2 * z + xi, pl.ds(lows[k], WIDTHS[k])],
                (((1,), (1,)), ((), ())), preferred_element_type=F32
            ).astype(BF16)

    b1_p, b1_m = ids.get("Bx1+", n), ids.get("Bx1-", n)
    b2n_p, b2n_m = ids.get("Bx2+n", n), ids.get("Bx2-n", n)
    b2a_p, b2a_m = ids.get("Bx2+a", n), ids.get("Bx2-a", n)
    z_p, z_m, z_o = ids.get("Bz+", n), ids.get("Bz-", n), ids.get("Bzo", n)
    fs, fz = ids.get("Fs", n), ids.get("Fz", 2 * n)
    fy = [ids.get(("Fy", d), 2 * n) for d in range(3)]
    fp = [ids.get(("Fp", d), n) for d in range(3)]
    id_u = ids.get("U", n)

    ys = (yR, yL, yO)
    sources = (yL, yR, yO)

    def brrows(k, f_):
        return brgs[k].at[pl.ds(pl.multiple_of(f_ * HALF, 16), HALF)]

    def f_spread(to, k):
        wait_recv(brrows(k, fO), fz + k)
        for d in range(3):
            send(to, lambda d=d: rc(brrows(k, fO), brrows(k, fO), fp[d] + k, fp[d] + k, dev(y_=ys[d])))

    def final(k):
        for d in range(3):
            wait_recv(brrows(k, zl * 4 + sources[d]), fy[d] + k)
            wait_recv(brrows(k, zlO * 4 + sources[d]), fp[d] + k)
        start = pl.multiple_of(c * 1792, 128)
        Us[k][c] = jnp.dot(QL[:, pl.ds(start, 1792)], brgs[k][...], preferred_element_type=F32)

    def final_send(to, k):
        send(to, lambda: rc(Us[k].at[c], Us[k].at[c], id_u + k, id_u + k, dev(core=oc)))

    def u_store(k, core):
        return pltpu.make_async_copy(
            Us[k].at[core], u_hbm.at[core, :, pl.ds(lows[k], WIDTHS[k])], lsem.at[6 + 2 * k + core])

    def finish(k):
        u_store(k, c).start()
        wait_recv(Us[k].at[oc], id_u + k)
        u_store(k, oc).start()

    def add_blocks(buf, first, count, terms):
        @pl.loop(0, count)
        def _(i):
            dst = buf.at[first + i]
            total = dst[...].astype(F32)
            for term in terms(i):
                total = total + term[...].astype(F32)
            dst[...] = total.astype(BF16)

    @pl.when(is_a)
    def _():
        xi_own, xi_opp = x // 2, 1 - x // 2

        def opp_sends(k):
            send(in_a, lambda: rc(Bs[k].at[pl.ds((1 - x // 2) * 4, 2)], Br1s[k].at[pl.ds(0, 2)],
                                  b1_p + k, b1_p + k, dev(x_=xR)))
            send(in_a, lambda: rc(Bs[k].at[pl.ds((1 - x // 2) * 4 + 2, 2)], Br1s[k].at[pl.ds(2, 2)],
                                  b1_m + k, b1_m + k, dev(x_=xL)))

        def block(k, z_):
            return Bs[k].at[(x // 2) * 4 + z_]

        def x_total(k):
            wait_recv(Br2s[k].at[0, pl.ds(2, 2)], b2n_p + k)
            wait_recv(Br2s[k].at[1, pl.ds(0, 2)], b2n_m + k)
            wait_recv(Br2s[k].at[0, pl.ds(0, 2)], b2a_p + k)
            wait_recv(Br2s[k].at[1, pl.ds(2, 2)], b2a_m + k)
            add_blocks(Bs[k], xi_own * 4, 4, lambda i: (Br2s[k].at[0, i], Br2s[k].at[1, i]))
            send(in_a, lambda: rc(block(k, zR), Zrs[k].at[0], z_p + k, z_p + k, dev(zh_=zR)))
            send(in_a, lambda: rc(block(k, zL), Zrs[k].at[1], z_m + k, z_m + k, dev(zh_=zL)))
            send(in_a, lambda: rc(block(k, zO), Zrs[k].at[2], z_o + k, z_o + k, dev(zh_=zO)))

        def z_total(k):
            wait_recv(Zrs[k].at[0], z_p + k)
            wait_recv(Zrs[k].at[1], z_m + k)
            wait_recv(Zrs[k].at[2], z_o + k)
            brs[k][...] = (Bs[k][(x // 2) * 4 + zh].astype(F32) + Zrs[k][0].astype(F32)
                           + Zrs[k][1].astype(F32) + Zrs[k][2].astype(F32)).astype(BF16)
            for other in range(2):
                def src(other=other):
                    return brs[k].at[half(oc if other else c)]

                def to(other=other, **moved):
                    return dev(core=oc if other else c, **moved)

                send(in_a, lambda src=src, to=to, other=other: rc(
                    src(), brrows(k, f), fz + k + n * other, fz + k, to(zl_=zlO)))
                for d in range(3):
                    send(in_a, lambda src=src, to=to, other=other, d=d: rc(
                        src(), brrows(k, f), fy[d] + k + n * other, fy[d] + k, to(y_=ys[d])))
            send(in_a, lambda: rc(brs[k].at[half(oc)], brrows(k, f), fs + k, fs + k, dev(core=oc)))
            brrows(k, f)[...] = brs[k][half(c), :]

        def start_chunk(k):
            multiply(k, xi_opp)
            opp_sends(k)
            multiply(k, xi_own)

        start_chunk(0)
        start_chunk(1)
        start_chunk(2)
        for k in range(n + 4):
            if k < n:
                x_total(k)
            if 0 <= k - 1 < n:
                z_total(k - 1)
            if k + 3 < n:
                start_chunk(k + 3)
            if 0 <= k - 2 < n:
                f_spread(in_a, k - 2)
            if 0 <= k - 3 < n:
                final(k - 3)
                final_send(in_a, k - 3)
            if 0 <= k - 4 < n:
                finish(k - 4)

    @pl.when(is_b)
    def _():
        xi_r, xi_l = xR // 2, xL // 2

        def x_send(first, x_, d, base, k):
            send(in_b, lambda: rc(Bs[k].at[pl.ds(x_ // 2 * 4 + first, 2)],
                                  Br2s[k].at[d, pl.ds(first, 2)], base + k, base + k, dev(x_=x_)))

        def plain_sends(k):
            x_send(2, xR, 0, b2n_p, k)
            x_send(0, xL, 1, b2n_m, k)

        def sum_sends(k):
            wait_recv(Br1s[k].at[pl.ds(0, 2)], b1_p + k)
            add_blocks(Bs[k], xi_r * 4, 2, lambda i: (Br1s[k].at[i],))
            x_send(0, xR, 0, b2a_p, k)
            wait_recv(Br1s[k].at[pl.ds(2, 2)], b1_m + k)
            add_blocks(Bs[k], xi_l * 4 + 2, 2, lambda i: (Br1s[k].at[2 + i],))
            x_send(2, xL, 1, b2a_m, k)

        def start_chunk(k):
            multiply(k, 0)
            multiply(k, 1)

        start_chunk(0)
        plain_sends(0)
        start_chunk(1)
        for k in range(n + 5):
            if k < n:
                sum_sends(k)
            if k + 1 < n:
                plain_sends(k + 1)
            if k + 2 < n:
                start_chunk(k + 2)
            if 0 <= k - 3 < n:
                f_spread(in_b, k - 3)
            if 0 <= k - 4 < n:
                wait_recv(brrows(k - 4, f), fs + k - 4)
                final(k - 4)
                final_send(in_b, k - 4)
            if 0 <= k - 5 < n:
                finish(k - 5)

    for build in common:
        build().wait_send()

    @pl.when(is_a)
    def _():
        for build in in_a:
            build().wait_send()

    @pl.when(is_b)
    def _():
        for build in in_b:
            build().wait_send()

    rot_store.wait()
    for k in chunks:
        for core in range(2):
            u_store(k, core).wait()
    assert ids.count <= SEMS, ids.count


SEMS = 260


def per_device(replica_grads, basis_left, basis_right, first_moment, second_moment):
    any_space = pl.BlockSpec(memory_space=pl.ANY)
    v = pltpu.VMEM
    scratch = [
        v((ROWS, COLS), BF16),
        v((HALF, COLS), BF16),
        v((HALF, COLS), BF16),
        v((HALF, COLS), BF16),
        v((8, ROWS, COLS), BF16),
        v((8, COLS, COLS), BF16),
        v((ROWS, 3584), BF16),
        v((1792, ROWS), BF16),
        v((ROWS, COLS), F32),
        v((ROWS, COLS - YF), BF16),
        v((ROWS, COLS - YF), BF16),
        v((ROWS, YF), BF16),
        v((ROWS, YF), BF16),
        v((ROWS, COLS), BF16),
        v((8 * HALF, YF), BF16),
        v((8 * HALF, COLS - YF), BF16),
        v((2, HALF, YF), BF16),
        v((2, 2, HALF, YF), BF16),
        v((HALF, YF), BF16),
        v((HALF, COLS), F32),
        v((HALF, YF), BF16),
        v((4, HALF, COLS - YF), BF16),
        v((2, SUB, COLS - YF), BF16),
        v((2, HALF, COLS - YF), BF16),
        v((HALF, COLS), F32),
        v((HALF, COLS), F32),
        v((ROWS, COLS), BF16),
        [v((8, ROWS, w), BF16) for w in WIDTHS],
        [v((4, ROWS, w), BF16) for w in WIDTHS],
        [v((2, 4, ROWS, w), BF16) for w in WIDTHS],
        [v((3, ROWS, w), BF16) for w in WIDTHS],
        [v((ROWS, w), BF16) for w in WIDTHS],
        [v((8 * HALF, w), BF16) for w in WIDTHS],
        [v((2, ROWS, w), F32) for w in WIDTHS],
        pltpu.SemaphoreType.DMA((SEMS,)),
        pltpu.SemaphoreType.DMA((SEMS,)),
        pltpu.SemaphoreType.DMA((6 + 2 * len(WIDTHS),)),
    ]
    rotated, partials = pl.pallas_call(
        kernel,
        out_shape=(
            jax.ShapeDtypeStruct((HALF, COLS), F32),
            jax.ShapeDtypeStruct((2, ROWS, COLS), F32),
        ),
        in_specs=[any_space] * 5,
        out_specs=(any_space,) * 2,
        scratch_shapes=scratch,
        compiler_params=pltpu.CompilerParams(
            collective_id=0, has_side_effects=True, vmem_limit_bytes=60 * 2**20
        ),
        cost_estimate=pl.CostEstimate(
            flops=9 * 10**9, bytes_accessed=10 * 2**20, transcendentals=HALF * COLS
        ),
        name="soap_step",
    )(replica_grads, basis_left, basis_right, first_moment, second_moment)
    first_next = beta_first * first_moment + (1.0 - beta_first) * rotated
    second_next = beta_second * second_moment + (1.0 - beta_second) * rotated * rotated
    return (first_next, second_next, partials[0] + partials[1])


def solution(mesh):
    placed = (
        P("dp", "fsdp", "tensor"),
        P("fsdp", None),
        P("fsdp", "tensor"),
        P(("dp", "fsdp"), "tensor"),
        P(("dp", "fsdp"), "tensor"),
    )
    return jax.shard_map(
        per_device,
        mesh=mesh,
        in_specs=placed,
        out_specs=(P(("dp", "fsdp"), "tensor"), P(("dp", "fsdp"), "tensor"), P("fsdp", "tensor")),
        check_vma=False,
    )
```

```python
import functools

import jax
import jax.numpy as jnp
from jax import lax
from jax.experimental import pallas as pl
from jax.experimental.pallas import tpu as pltpu
from jax.sharding import PartitionSpec as P

MESH = pl.DeviceIdType.MESH
F32 = jnp.float32
BF16 = jnp.bfloat16

ADAM_STEP = 10
beta_first = 0.9
beta_second = 0.95
epsilon = 1e-08

ROWS = 448
HALF = 224
COLS = 640
SUB = 112
YF = 384
WIDTHS = (128, 128, 128, 128, 128)


class Ids:
    def __init__(self):
        self.table = {}
        self.count = 0

    def get(self, name, width=1):
        if name not in self.table:
            self.table[name] = self.count
            self.count += width
        return self.table[name]


def kernel(
    g_hbm, ql_hbm, qr_hbm, m1_hbm, m2_hbm,
    rot_hbm, u_hbm,
    gv, gx, gs, Gq, G, Q, QL, QT, T, Tse, Tre, Tsl, Trl, Tb, P0, P1, Pr1, Pr2, Rs, Rf, Rr, Zp, Sy1, Sy2,
    m1, m2, D, Bs, Br1s, Br2s, Zrs, brs, brgs, Us,
    ssem, rsem, lsem,
):
    ids = Ids()
    c = lax.axis_index("dp")
    f = lax.axis_index("fsdp")
    t = lax.axis_index("tensor")
    zl, y = f // 4, f % 4
    zh, x = t // 4, t % 4
    p = x % 2
    is_a = c == p
    is_b = c != p
    oc = 1 - c
    yR, yL, yO = (y + 1) % 4, (y + 3) % 4, (y + 2) % 4
    xR, xL, xO = (x + 1) % 4, (x + 3) % 4, (x + 2) % 4
    zR, zL, zO = (zh + 1) % 4, (zh + 3) % 4, (zh + 2) % 4
    zlO = 1 - zl
    fO = zlO * 4 + y

    def dev(core=c, zl_=zl, y_=y, zh_=zh, x_=x):
        return (core, zl_ * 4 + y_, zh_ * 4 + x_)

    def rc(src, dst, sid, rid, device):
        return pltpu.make_async_remote_copy(
            src_ref=src, dst_ref=dst, send_sem=ssem.at[sid], recv_sem=rsem.at[rid],
            device_id=device, device_id_type=MESH,
        )

    common, in_a, in_b = [], [], []

    def send(to, build):
        build().start()
        to.append(build)

    def wait_recv(dst, rid):
        rc(dst, dst, 0, rid, dev(core=oc)).wait_recv()

    def half(h):
        return pl.ds(pl.multiple_of(h * HALF, 16), HALF)

    qr_load = pltpu.make_async_copy(
        qr_hbm.at[pl.ds(pl.multiple_of(c * COLS, COLS), COLS)], Q.at[f], lsem.at[0])
    g_load = pltpu.make_async_copy(g_hbm.at[0], gv, lsem.at[1])
    ql_load = pltpu.make_async_copy(ql_hbm, QL, lsem.at[2])
    m1_load = pltpu.make_async_copy(m1_hbm, m1, lsem.at[3])
    m2_load = pltpu.make_async_copy(m2_hbm, m2, lsem.at[4])
    g_load.start()
    qr_load.start()
    ql_load.start()
    m1_load.start()
    m2_load.start()

    barrier = pltpu.get_barrier_semaphore()
    friends = [dev(core=oc), dev(zh_=zO)]
    for core in (c, oc):
        friends += [dev(core=core, x_=xR), dev(core=core, x_=xL), dev(core=core, y_=yR), dev(core=core, y_=yL), dev(core=core, zl_=zlO),
                    dev(core=core, zh_=zR), dev(core=core, zh_=zL)]
    for friend in friends:
        pl.semaphore_signal(barrier, inc=1, device_id=friend, device_id_type=MESH)
    pl.semaphore_wait(barrier, len(friends))

    g_load.wait()
    send(common, lambda: rc(gv.at[half(oc)], gx, ids.get("g"), ids.get("g"), dev(core=oc)))
    qr_load.wait()

    def qpart(slot, a):
        return Q.at[slot, pl.ds(a * 320, 320)]

    def qsend(name, slot, a, device):
        i = ids.get(name)
        send(common, lambda: rc(qpart(slot, a), qpart(slot, a), i, i, device))

    def qy_own(a):
        qsend(("Qy+", "own", a), f, a, dev(y_=yR))
        qsend(("Qy-", "own", a), f, a, dev(y_=yL))

    def qz_send(a):
        qsend(("Qz", a), f, a, dev(zl_=zlO))

    qy_own(0)
    qz_send(0)
    qy_own(1)

    wait_recv(gx, ids.get("g"))
    gs[...] = (gv[half(c), :].astype(F32) + gx[...].astype(F32)).astype(BF16)

    own = 2 * zh + x // 2

    def gpart(slot, h):
        return G.at[slot, half(h)]

    gz_p, gz_m, gz_o = ids.get("Gz+", 2), ids.get("Gz-", 2), ids.get("Gzo", 2)
    send(common, lambda: rc(gs, gpart(own, c), gz_p + c, gz_p + c, dev(core=p, zh_=zR)))
    send(common, lambda: rc(gs, gpart(own, c), gz_m + c, gz_m + c, dev(core=p, zh_=zL)))
    gx_p, gx_m = ids.get("Gx+", 8), ids.get("Gx-", 8)
    zq = [zh, zL, zR, zO]
    gf_p, gf_m = ids.get("Gxf+", 4), ids.get("Gxf-", 4)
    id_gs, id_gs3 = ids.get("Gs"), ids.get("Gs3")

    def gslot(q, x_):
        return 2 * zq[q] + x_ // 2

    def a_spread(q, h, src=None):
        for base, x_ in ((gx_p, xR), (gx_m, xL)):
            send(in_a, lambda base=base, x_=x_: rc(
                gpart(gslot(q, x), h) if src is None else src, gpart(gslot(q, x), h),
                base + 2 * q + h, base + 2 * q + h, dev(x_=x_)))

    def b_spread(q, src):
        for base, x_ in ((gx_p, xR), (gx_m, xL)):
            send(in_b, lambda base=base, x_=x_: rc(
                src, gpart(gslot(q, x), c), base + 2 * q + c, base + 2 * q + c, dev(core=oc, x_=x_)))

    def qy_own_forward():
        i = ids.get(("Qy+", "own", 0))
        wait_recv(qpart(zl * 4 + yL, 0), i)
        qsend(("Qyf+", "own"), zl * 4 + yL, 0, dev(y_=yR))
        i = ids.get(("Qy-", "own", 1))
        wait_recv(qpart(zl * 4 + yR, 1), i)
        qsend(("Qyf-", "own"), zl * 4 + yR, 1, dev(y_=yL))

    def qz_spread(a):
        wait_recv(qpart(fO, a), ids.get(("Qz", a)))
        qsend(("Qy+", "par", a), fO, a, dev(y_=yR))
        qsend(("Qy-", "par", a), fO, a, dev(y_=yL))

    def transpose_left(group):
        start = pl.multiple_of(c * 1792 + group * 896, 128)
        QT[pl.ds(group * 896, 896), :] = QL[:, pl.ds(start, 896)].T

    def qz_opposite():
        wait_recv(qpart(zl * 4 + yO, 1), ids.get(("Qyf-", "own")))
        i = ids.get("Qzo")
        send(common, lambda: rc(qpart(zl * 4 + yO, 1), qpart(zl * 4 + yO, 1), i, i, dev(zl_=zlO)))

    def quarter(slot, a):
        return Q.at[slot, pl.ds(a * 160, 160)]

    def qy_par_forward():
        wait_recv(qpart(zlO * 4 + yL, 0), ids.get(("Qy+", "par", 0)))
        i = ids.get(("Qyf+", "par"))
        send(common, lambda: rc(quarter(zlO * 4 + yL, 0), quarter(zlO * 4 + yL, 0), i, i, dev(y_=yR)))
        wait_recv(qpart(zlO * 4 + yR, 0), ids.get(("Qy-", "par", 0)))
        j = ids.get(("Qyf-", "par"))
        send(common, lambda: rc(quarter(zlO * 4 + yR, 1), quarter(zlO * 4 + yR, 1), j, j, dev(y_=yL)))

    def b_forward(q, h):
        if h == 0:
            wait_recv(gpart(gslot(q, xL), 0), gx_p + 2 * q)
            send(in_b, lambda: rc(gpart(gslot(q, xL), 0), gpart(gslot(q, xL), 0), gf_p + q, gf_p + q, dev(x_=xR)))
        else:
            wait_recv(gpart(gslot(q, xR), 1), gx_m + 2 * q + 1)
            send(in_b, lambda: rc(gpart(gslot(q, xR), 1), gpart(gslot(q, xR), 1), gf_m + q, gf_m + q, dev(x_=xL)))

    @pl.when(is_a)
    def _():
        send(in_a, lambda: rc(gs, gpart(own, c), gz_o + c, gz_o + c, dev(zh_=zO)))
        a_spread(0, c, src=gs)
        G[own, half(c), :] = gs[...]
        wait_recv(gpart(gslot(1, x), 0), gz_p + 0)
        a_spread(1, 0)
        wait_recv(gpart(gslot(2, x), 1), gz_m + 1)
        a_spread(2, 1)

    @pl.when(is_b)
    def _():
        send(in_b, lambda: rc(gs, Gq, gz_o + c, gz_o + c, dev(zh_=zO)))
        b_spread(0, gs)
        send(in_b, lambda: rc(gs, gpart(own, c), id_gs, id_gs, dev(core=oc)))
        b_forward(0, 0)
        b_forward(0, 1)

    qz_send(1)
    ql_load.wait()
    transpose_left(0)

    @pl.when(is_a)
    def _():
        wait_recv(gpart(gslot(1, x), 1), gz_p + 1)
        a_spread(1, 1)
        wait_recv(gpart(gslot(2, x), 0), gz_m + 0)
        a_spread(2, 0)

    qy_own_forward()

    @pl.when(is_a)
    def _():
        wait_recv(gpart(gslot(3, x), c), gz_o + c)
        a_spread(3, c)

    @pl.when(is_b)
    def _():
        b_forward(1, 0)
        wait_recv(Gq, gz_o + c)
        b_spread(3, Gq)
        send(in_b, lambda: rc(Gq, gpart(gslot(3, x), c), id_gs3, id_gs3, dev(core=oc)))
        b_forward(2, 1)

    qz_spread(0)

    @pl.when(is_b)
    def _():
        b_forward(1, 1)
        b_forward(2, 0)

    qz_spread(1)
    transpose_left(1)

    @pl.when(is_b)
    def _():
        b_forward(3, 0)
        b_forward(3, 1)

    qz_opposite()
    qy_par_forward()

    @pl.when(is_b)
    def _():
        for q in range(4):
            wait_recv(gpart(gslot(q, xL), 1), gx_p + 2 * q + 1)
            wait_recv(gpart(gslot(q, xR), 0), gx_m + 2 * q)

    @pl.when(is_a)
    def _():
        wait_recv(gpart(own, oc), id_gs)
        wait_recv(gpart(gslot(3, x), oc), id_gs3)
        for q in range(4):
            wait_recv(gpart(gslot(q, xO), 0), gf_p + q)
            wait_recv(gpart(gslot(q, xO), 1), gf_m + q)

    def psend(name, src, dst, device):
        i = ids.get(name)
        send(common, lambda: rc(src, dst, i, i, device))

    T[...] = jnp.zeros_like(T)
    last = zlO * 4 + yO

    def accumulate(slot):
        T[...] += jnp.dot(G[slot], Q[slot], preferred_element_type=F32)

    wait_recv(qpart(zl * 4 + yL, 1), ids.get(("Qy+", "own", 1)))
    wait_recv(qpart(zl * 4 + yR, 0), ids.get(("Qy-", "own", 0)))
    wait_recv(qpart(zl * 4 + yO, 0), ids.get(("Qyf+", "own")))

    @pl.loop(0, 4)
    def _(i):
        accumulate(zl * 4 + i)

    accumulate(fO)
    wait_recv(qpart(zlO * 4 + yL, 1), ids.get(("Qy+", "par", 1)))
    wait_recv(qpart(zlO * 4 + yR, 1), ids.get(("Qy-", "par", 1)))

    @pl.loop(0, 2)
    def _(i):
        accumulate(zlO * 4 + (y + 1 + 2 * i) % 4)

    wait_recv(quarter(last, 0), ids.get(("Qyf+", "par")))
    wait_recv(quarter(last, 1), ids.get(("Qyf-", "par")))
    wait_recv(qpart(last, 1), ids.get("Qzo"))
    early, late = slice(YF, COLS), slice(0, YF)
    for cols, buf, got, name in ((early, Tse, Tre, "Te"), (late, Tsl, Trl, "Tl")):
        T[:, cols] += jnp.dot(G[last], Q[last, :, cols], preferred_element_type=F32)
        buf[...] = T[:, cols].astype(BF16)
        psend(name, buf, got, dev(core=oc))

    def exchanged(got, cols, name):
        wait_recv(got, ids.get(name))
        Tb[:, cols] = (T[:, cols] + got[...].astype(F32)).astype(BF16)

    def left(buf, group, lo, width):
        r = pl.ds(pl.multiple_of(group * 896, 128), 896)
        buf[r, :] = jnp.dot(
            QT[r, :], Tb[:, lo:lo + width], preferred_element_type=F32).astype(BF16)

    def pblock(buf, zl_, y_):
        return buf.at[pl.ds(pl.multiple_of((zl_ * 4 + y_) * HALF, 16), HALF)]

    def spart(y_, s):
        return P1.at[pl.ds(pl.multiple_of((zl * 4 + y_) * HALF + s * SUB, 16), SUB)]

    def half_of(buf, s):
        return buf.at[pl.ds(s * SUB, SUB)]

    def add_into(dst, *others):
        total = dst[...].astype(F32)
        for other in others:
            total = total + other[...].astype(F32)
        dst[...] = total.astype(dst.dtype)

    exchanged(Tre, early, "Te")
    left(P1, zlO, YF, COLS - YF)
    for name, y_ in (("O", yO), ("R", yR), ("L", yL), ("S", y)):
        psend(("Pz1", name), pblock(P1, zlO, y_), Zp.at[y_], dev(zl_=zlO))
    exchanged(Trl, late, "Tl")
    left(P0, 0, 0, YF)
    psend("Py1+", pblock(P0, 0, yO), Pr1.at[0], dev(y_=yR))
    psend("Py2-n", pblock(P0, 0, yL), Pr2.at[1, 0], dev(y_=yL))
    left(P0, 1, 0, YF)
    psend("Py1-", pblock(P0, 1, yO), Pr1.at[1], dev(y_=yL))
    psend("Py2+n", pblock(P0, 1, yR), Pr2.at[0, 1], dev(y_=yR))
    left(P1, zl, YF, COLS - YF)

    def z_add(name, y_):
        wait_recv(Zp.at[y_], ids.get(("Pz1", name)))
        add_into(pblock(P1, zl, y_), Zp.at[y_])

    z_add("O", yO)
    psend("Sy1+", spart(yO, 0), Sy1.at[0], dev(y_=yR))
    psend("Sy1-", spart(yO, 1), Sy1.at[1], dev(y_=yL))
    wait_recv(Pr1.at[0], ids.get("Py1+"))
    add_into(pblock(P0, 0, yR), Pr1.at[0])
    psend("Py2+a", pblock(P0, 0, yR), Pr2.at[0, 0], dev(y_=yR))
    wait_recv(Pr1.at[1], ids.get("Py1-"))
    add_into(pblock(P0, 1, yL), Pr1.at[1])
    psend("Py2-a", pblock(P0, 1, yL), Pr2.at[1, 1], dev(y_=yL))
    z_add("R", yR)
    psend("Sy2+n", spart(yR, 1), half_of(Sy2.at[0], 1), dev(y_=yR))
    wait_recv(Sy1.at[0], ids.get("Sy1+"))
    add_into(spart(yR, 0), Sy1.at[0])
    psend("Sy2+a", spart(yR, 0), half_of(Sy2.at[0], 0), dev(y_=yR))
    z_add("L", yL)
    psend("Sy2-n", spart(yL, 0), half_of(Sy2.at[1], 0), dev(y_=yL))
    wait_recv(Sy1.at[1], ids.get("Sy1-"))
    add_into(spart(yL, 1), Sy1.at[1])
    psend("Sy2-a", spart(yL, 1), half_of(Sy2.at[1], 1), dev(y_=yL))
    wait_recv(Pr2.at[0, 1], ids.get("Py2+n"))
    wait_recv(Pr2.at[1, 0], ids.get("Py2-n"))
    wait_recv(Pr2.at[0, 0], ids.get("Py2+a"))
    wait_recv(Pr2.at[1, 1], ids.get("Py2-a"))

    def block_total(zl_):
        return (pblock(P0, zl_, y)[...].astype(F32) + Pr2[0, zl_].astype(F32)
                + Pr2[1, zl_].astype(F32))

    Rs[...] = block_total(zlO).astype(BF16)
    psend("Pz", Rs, Rr, dev(zl_=zlO))
    Rf[:, 0:YF] = block_total(zl)
    wait_recv(Zp.at[y], ids.get(("Pz1", "S")))
    total = pblock(P1, zl, y)[...].astype(F32) + Zp[y].astype(F32)
    wait_recv(half_of(Sy2.at[0], 0), ids.get("Sy2+a"))
    wait_recv(half_of(Sy2.at[0], 1), ids.get("Sy2+n"))
    wait_recv(half_of(Sy2.at[1], 0), ids.get("Sy2-n"))
    wait_recv(half_of(Sy2.at[1], 1), ids.get("Sy2-a"))
    Rf[:, YF:COLS] = total + Sy2[0].astype(F32) + Sy2[1].astype(F32)
    m1_load.wait()
    m2_load.wait()
    wait_recv(Rr, ids.get("Pz"))

    def adam(r, lo, hi, rotated):
        Rf[r, lo:hi] = rotated
        first = beta_first * m1[r, lo:hi] + (1.0 - beta_first) * rotated
        second = beta_second * m2[r, lo:hi] + (1.0 - beta_second) * rotated * rotated
        first_hat = first / (1.0 - beta_first**ADAM_STEP)
        second_hat = second / (1.0 - beta_second**ADAM_STEP)
        where = pl.ds(pl.multiple_of(c * HALF + r.start, 16), 32)
        D[where, lo:hi] = (first_hat / (jnp.sqrt(second_hat) + epsilon)).astype(BF16)

    @pl.loop(0, HALF // 32)
    def _(i):
        r = pl.ds(pl.multiple_of(i * 32, 32), 32)
        adam(r, 0, YF, Rf[r, 0:YF] + Rr[r, :].astype(F32))
        adam(r, YF, COLS, Rf[r, YF:COLS])

    id_d = ids.get("D")
    send(common, lambda: rc(D.at[half(c)], D.at[half(c)], id_d, id_d, dev(core=oc)))
    rot_store = pltpu.make_async_copy(Rf, rot_hbm, lsem.at[5])
    rot_store.start()
    wait_recv(D.at[half(oc)], id_d)

    chunks = range(len(WIDTHS))
    lows = [sum(WIDTHS[:k]) for k in chunks]
    n = len(WIDTHS)

    def multiply(k, xi):
        @pl.loop(0, 4)
        def _(z):
            Bs[k][xi * 4 + z] = lax.dot_general(
                D[...], Q[2 * z + xi, pl.ds(lows[k], WIDTHS[k])],
                (((1,), (1,)), ((), ())), preferred_element_type=F32
            ).astype(BF16)

    b1_p, b1_m = ids.get("Bx1+", n), ids.get("Bx1-", n)
    b2n_p, b2n_m = ids.get("Bx2+n", n), ids.get("Bx2-n", n)
    b2a_p, b2a_m = ids.get("Bx2+a", n), ids.get("Bx2-a", n)
    z_p, z_m, z_o = ids.get("Bz+", n), ids.get("Bz-", n), ids.get("Bzo", n)
    fs, fz = ids.get("Fs", n), ids.get("Fz", 2 * n)
    fy = [ids.get(("Fy", d), 2 * n) for d in range(3)]
    fp = [ids.get(("Fp", d), n) for d in range(3)]
    id_u = ids.get("U", n)

    ys = (yR, yL, yO)
    sources = (yL, yR, yO)

    def brrows(k, f_):
        return brgs[k].at[pl.ds(pl.multiple_of(f_ * HALF, 16), HALF)]

    def f_spread(to, k):
        wait_recv(brrows(k, fO), fz + k)
        for d in range(3):
            send(to, lambda d=d: rc(brrows(k, fO), brrows(k, fO), fp[d] + k, fp[d] + k, dev(y_=ys[d])))

    def final(k):
        for d in range(3):
            wait_recv(brrows(k, zl * 4 + sources[d]), fy[d] + k)
            wait_recv(brrows(k, zlO * 4 + sources[d]), fp[d] + k)
        start = pl.multiple_of(c * 1792, 128)
        Us[k][c] = jnp.dot(QL[:, pl.ds(start, 1792)], brgs[k][...], preferred_element_type=F32)

    def final_send(to, k):
        send(to, lambda: rc(Us[k].at[c], Us[k].at[c], id_u + k, id_u + k, dev(core=oc)))

    def u_store(k, core):
        return pltpu.make_async_copy(
            Us[k].at[core], u_hbm.at[core, :, pl.ds(lows[k], WIDTHS[k])], lsem.at[6 + 2 * k + core])

    def finish(k):
        u_store(k, c).start()
        wait_recv(Us[k].at[oc], id_u + k)
        u_store(k, oc).start()

    def add_blocks(buf, first, count, terms):
        @pl.loop(0, count)
        def _(i):
            dst = buf.at[first + i]
            total = dst[...].astype(F32)
            for term in terms(i):
                total = total + term[...].astype(F32)
            dst[...] = total.astype(BF16)

    @pl.when(is_a)
    def _():
        xi_own, xi_opp = x // 2, 1 - x // 2

        def opp_sends(k):
            send(in_a, lambda: rc(Bs[k].at[pl.ds((1 - x // 2) * 4, 2)], Br1s[k].at[pl.ds(0, 2)],
                                  b1_p + k, b1_p + k, dev(x_=xR)))
            send(in_a, lambda: rc(Bs[k].at[pl.ds((1 - x // 2) * 4 + 2, 2)], Br1s[k].at[pl.ds(2, 2)],
                                  b1_m + k, b1_m + k, dev(x_=xL)))

        def block(k, z_):
            return Bs[k].at[(x // 2) * 4 + z_]

        def x_total(k):
            wait_recv(Br2s[k].at[0, pl.ds(2, 2)], b2n_p + k)
            wait_recv(Br2s[k].at[1, pl.ds(0, 2)], b2n_m + k)
            wait_recv(Br2s[k].at[0, pl.ds(0, 2)], b2a_p + k)
            wait_recv(Br2s[k].at[1, pl.ds(2, 2)], b2a_m + k)
            add_blocks(Bs[k], xi_own * 4, 4, lambda i: (Br2s[k].at[0, i], Br2s[k].at[1, i]))
            send(in_a, lambda: rc(block(k, zR), Zrs[k].at[0], z_p + k, z_p + k, dev(zh_=zR)))
            send(in_a, lambda: rc(block(k, zL), Zrs[k].at[1], z_m + k, z_m + k, dev(zh_=zL)))
            send(in_a, lambda: rc(block(k, zO), Zrs[k].at[2], z_o + k, z_o + k, dev(zh_=zO)))

        def z_total(k):
            wait_recv(Zrs[k].at[0], z_p + k)
            wait_recv(Zrs[k].at[1], z_m + k)
            wait_recv(Zrs[k].at[2], z_o + k)
            brs[k][...] = (Bs[k][(x // 2) * 4 + zh].astype(F32) + Zrs[k][0].astype(F32)
                           + Zrs[k][1].astype(F32) + Zrs[k][2].astype(F32)).astype(BF16)
            for other in range(2):
                def src(other=other):
                    return brs[k].at[half(oc if other else c)]

                def to(other=other, **moved):
                    return dev(core=oc if other else c, **moved)

                send(in_a, lambda src=src, to=to, other=other: rc(
                    src(), brrows(k, f), fz + k + n * other, fz + k, to(zl_=zlO)))
                for d in range(3):
                    send(in_a, lambda src=src, to=to, other=other, d=d: rc(
                        src(), brrows(k, f), fy[d] + k + n * other, fy[d] + k, to(y_=ys[d])))
            send(in_a, lambda: rc(brs[k].at[half(oc)], brrows(k, f), fs + k, fs + k, dev(core=oc)))
            brrows(k, f)[...] = brs[k][half(c), :]

        def start_chunk(k):
            multiply(k, xi_opp)
            opp_sends(k)
            multiply(k, xi_own)

        start_chunk(0)
        start_chunk(1)
        start_chunk(2)
        for k in range(n + 4):
            if k < n:
                x_total(k)
            if 0 <= k - 1 < n:
                z_total(k - 1)
            if k + 3 < n:
                start_chunk(k + 3)
            if 0 <= k - 2 < n:
                f_spread(in_a, k - 2)
            if 0 <= k - 3 < n:
                final(k - 3)
                final_send(in_a, k - 3)
            if 0 <= k - 4 < n:
                finish(k - 4)

    @pl.when(is_b)
    def _():
        xi_r, xi_l = xR // 2, xL // 2

        def x_send(first, x_, d, base, k):
            send(in_b, lambda: rc(Bs[k].at[pl.ds(x_ // 2 * 4 + first, 2)],
                                  Br2s[k].at[d, pl.ds(first, 2)], base + k, base + k, dev(x_=x_)))

        def plain_sends(k):
            x_send(2, xR, 0, b2n_p, k)
            x_send(0, xL, 1, b2n_m, k)

        def sum_sends(k):
            wait_recv(Br1s[k].at[pl.ds(0, 2)], b1_p + k)
            add_blocks(Bs[k], xi_r * 4, 2, lambda i: (Br1s[k].at[i],))
            x_send(0, xR, 0, b2a_p, k)
            wait_recv(Br1s[k].at[pl.ds(2, 2)], b1_m + k)
            add_blocks(Bs[k], xi_l * 4 + 2, 2, lambda i: (Br1s[k].at[2 + i],))
            x_send(2, xL, 1, b2a_m, k)

        def start_chunk(k):
            multiply(k, 0)
            multiply(k, 1)

        start_chunk(0)
        plain_sends(0)
        start_chunk(1)
        start_chunk(2)
        for k in range(n + 5):
            if k < n:
                sum_sends(k)
            if k + 1 < n:
                plain_sends(k + 1)
            if k + 3 < n:
                start_chunk(k + 3)
            if 0 <= k - 3 < n:
                f_spread(in_b, k - 3)
            if 0 <= k - 4 < n:
                wait_recv(brrows(k - 4, f), fs + k - 4)
                final(k - 4)
                final_send(in_b, k - 4)
            if 0 <= k - 5 < n:
                finish(k - 5)

    for build in common:
        build().wait_send()

    @pl.when(is_a)
    def _():
        for build in in_a:
            build().wait_send()

    @pl.when(is_b)
    def _():
        for build in in_b:
            build().wait_send()

    rot_store.wait()
    for k in chunks:
        for core in range(2):
            u_store(k, core).wait()
    assert ids.count <= SEMS, ids.count


SEMS = 260


def per_device(replica_grads, basis_left, basis_right, first_moment, second_moment):
    any_space = pl.BlockSpec(memory_space=pl.ANY)
    v = pltpu.VMEM
    scratch = [
        v((ROWS, COLS), BF16),
        v((HALF, COLS), BF16),
        v((HALF, COLS), BF16),
        v((HALF, COLS), BF16),
        v((8, ROWS, COLS), BF16),
        v((8, COLS, COLS), BF16),
        v((ROWS, 3584), BF16),
        v((1792, ROWS), BF16),
        v((ROWS, COLS), F32),
        v((ROWS, COLS - YF), BF16),
        v((ROWS, COLS - YF), BF16),
        v((ROWS, YF), BF16),
        v((ROWS, YF), BF16),
        v((ROWS, COLS), BF16),
        v((8 * HALF, YF), BF16),
        v((8 * HALF, COLS - YF), BF16),
        v((2, HALF, YF), BF16),
        v((2, 2, HALF, YF), BF16),
        v((HALF, YF), BF16),
        v((HALF, COLS), F32),
        v((HALF, YF), BF16),
        v((4, HALF, COLS - YF), BF16),
        v((2, SUB, COLS - YF), BF16),
        v((2, HALF, COLS - YF), BF16),
        v((HALF, COLS), F32),
        v((HALF, COLS), F32),
        v((ROWS, COLS), BF16),
        [v((8, ROWS, w), BF16) for w in WIDTHS],
        [v((4, ROWS, w), BF16) for w in WIDTHS],
        [v((2, 4, ROWS, w), BF16) for w in WIDTHS],
        [v((3, ROWS, w), BF16) for w in WIDTHS],
        [v((ROWS, w), BF16) for w in WIDTHS],
        [v((8 * HALF, w), BF16) for w in WIDTHS],
        [v((2, ROWS, w), F32) for w in WIDTHS],
        pltpu.SemaphoreType.DMA((SEMS,)),
        pltpu.SemaphoreType.DMA((SEMS,)),
        pltpu.SemaphoreType.DMA((6 + 2 * len(WIDTHS),)),
    ]
    rotated, partials = pl.pallas_call(
        kernel,
        out_shape=(
            jax.ShapeDtypeStruct((HALF, COLS), F32),
            jax.ShapeDtypeStruct((2, ROWS, COLS), F32),
        ),
        in_specs=[any_space] * 5,
        out_specs=(any_space,) * 2,
        scratch_shapes=scratch,
        compiler_params=pltpu.CompilerParams(
            collective_id=0, has_side_effects=True, vmem_limit_bytes=60 * 2**20
        ),
        cost_estimate=pl.CostEstimate(
            flops=9 * 10**9, bytes_accessed=10 * 2**20, transcendentals=HALF * COLS
        ),
        name="soap_step",
    )(replica_grads, basis_left, basis_right, first_moment, second_moment)
    first_next = beta_first * first_moment + (1.0 - beta_first) * rotated
    second_next = beta_second * second_moment + (1.0 - beta_second) * rotated * rotated
    return (first_next, second_next, partials[0] + partials[1])


def solution(mesh):
    placed = (
        P("dp", "fsdp", "tensor"),
        P("fsdp", None),
        P("fsdp", "tensor"),
        P(("dp", "fsdp"), "tensor"),
        P(("dp", "fsdp"), "tensor"),
    )
    return jax.shard_map(
        per_device,
        mesh=mesh,
        in_specs=placed,
        out_specs=(P(("dp", "fsdp"), "tensor"), P(("dp", "fsdp"), "tensor"), P("fsdp", "tensor")),
        check_vma=False,
    )
```
